128 devices in a mesh: dp: 8 (over x, y_hi), seq: 16 (over z, y_lo, core).
Axes of the slice: x: 4, y: 4 (y_hi: 2, y_lo: 2; y = y_hi * 2 + y_lo), z: 4, core: 2. Of those that a mesh axis runs over, the one named last changes fastest.
Arguments:
- tokens: bfloat16 [8, 8192, 2048], P('dp', 'seq'), may hold values from -6 to 6
- w_query: bfloat16 [2048, 1024], replicated, may hold values from -0.125 to 0.125
- keys: bfloat16 [8, 8192, 1024], P('dp', 'seq'), may hold values from -0.5 to 0.5
- values: bfloat16 [8, 8192, 1024], P('dp', 'seq'), may hold values from -6 to 6
- log_decay: float32 [8, 8, 8192], P('dp', None, 'seq'), may hold values from -0.76640625 to 0, as said below
- regular: float32 [8], replicated, may hold values from 1 to 8
- grad_out: bfloat16 [8, 8192, 1024], P('dp', 'seq'), may hold values from -0.0234375 to 0.0234375
Outputs:
- mixed: bfloat16 [8, 8192, 1024], P('dp', 'seq')
- query_grad: float32 [1024, 2048], P('dp', 'seq')
The draws below stay inside these ranges and needn't reach their ends.
Inputs may be any that keep to these rules, and one draw needn't show every extreme that they name: `log_decay`: a head's decay varies from position to position.
All inputs are finite; a program needn't handle non-finite values.
Results may differ from the reference program's by a relative error of at most 0.0049.
Values sent between devices are 32-bit elements; how exact they have to be, the bound alone decides.
A program may use at most 64 MiB of HBM per device.

```python
import math
import jax
import jax.numpy as jnp
from jax import lax

D = 2048
H = 8
DH = 128
GROUP = 512
ITERS = 4
BATCH_SEQUENCES = 8
SEQUENCE_LENGTH = 8192
HD = 1024


def draw_log_decay(key, part):
    sequence_lanes = jax.random.split(key, 6)
    fast_share = 0.5
    head_shape = (BATCH_SEQUENCES, H, 1)
    is_fast = jax.random.uniform(sequence_lanes[0], head_shape) < fast_share
    fast_rate = jnp.exp(jax.random.uniform(sequence_lanes[1], head_shape, minval=math.log(10.0), maxval=math.log(17.0))) / GROUP
    slow_rate = jnp.exp(jax.random.uniform(sequence_lanes[2], head_shape, minval=math.log(0.02), maxval=math.log(0.3))) / SEQUENCE_LENGTH
    event_rate = jnp.where(is_fast, fast_rate, slow_rate)
    random_offset = jnp.exp(jax.random.uniform(sequence_lanes[3], (BATCH_SEQUENCES, H, SEQUENCE_LENGTH), minval=-math.log(2.0), maxval=math.log(2.0)))
    spike_position = jax.random.randint(sequence_lanes[4], (BATCH_SEQUENCES, 2, 1), 0, SEQUENCE_LENGTH)
    token_positions = jnp.arange(SEQUENCE_LENGTH)
    spike_mask = jnp.any(token_positions[None, None, :] == spike_position, axis=1)
    portion_value = jax.random.uniform(sequence_lanes[5], (BATCH_SEQUENCES, H, SEQUENCE_LENGTH), minval=0.2, maxval=0.5)
    spike_event = jnp.where(spike_mask[:, None, :], -jnp.log(1.0 - portion_value), 0.0)
    return (-(event_rate * random_offset) - spike_event).astype(jnp.float32)


def shard_levels(stream_key, shape, cuts, least, largest):
    level, own = 1.0, jax.random.fold_in(stream_key, 6)
    for axis_at, parts in cuts:
        steps = jnp.exp(jax.random.uniform(jax.random.fold_in(own, axis_at), (parts,), jnp.float32, least / len(cuts), largest / len(cuts)))
        level = level * jnp.repeat(steps, shape[axis_at] // parts).reshape([-1 if axis == axis_at else 1 for axis in range(len(shape))])
    return level


def centred(own_key, extent, scale, bound, shards=(), held_as=jnp.bfloat16):
    entries = scale * jax.random.normal(own_key, extent, jnp.float32)
    if shards:
        entries = entries * shard_levels(own_key, extent, shards, -0.22, 0.18)
    return jnp.clip(entries, -bound, bound).astype(held_as)


def setup_inputs(seed: int = 0) -> dict:
    splits = jax.random.split(jax.random.key(seed), 8)
    return {
        "tokens": centred(splits[0], (BATCH_SEQUENCES, SEQUENCE_LENGTH, D), 1.0, 6.0, ((0, 8), (1, 16))),
        "w_query": centred(splits[1], (D, HD), D ** -0.5, 0.125),
        "keys": centred(splits[2], (BATCH_SEQUENCES, SEQUENCE_LENGTH, HD), DH ** -0.5, 0.5, ((0, 8), (1, 16))),
        "values": centred(splits[3], (BATCH_SEQUENCES, SEQUENCE_LENGTH, HD), 1.0, 6.0, ((0, 8), (1, 16))),
        "log_decay": draw_log_decay(jax.random.fold_in(splits[7], 71), 0),
        "regular": jnp.clip(jnp.exp(jax.random.uniform(splits[5], (H,), jnp.float32, math.log(1.0), math.log(8.0))), 1.0, 8.0),
        "grad_out": centred(splits[6], (BATCH_SEQUENCES, SEQUENCE_LENGTH, HD), (BATCH_SEQUENCES * SEQUENCE_LENGTH) ** -0.5, 0.0234375, ((0, 8), (1, 16))),
    }


exact_mode = lax.Precision.HIGHEST


def product(left, right):
    return jnp.dot(left, right, precision=exact_mode)


def decay_table(cumulative):
    token_positions = jnp.arange(cumulative.shape[0])
    lower_mask = token_positions[:, None] >= token_positions[None, :]
    spread = cumulative[:, None] - cumulative[None, :]
    return jnp.where(lower_mask, jnp.exp(jnp.where(lower_mask, spread, 0.0)), 0.0)


def chebyshev(right_side, apply_fn, center, half_span):
    solution = jnp.zeros_like(right_side)
    residual = right_side
    search = right_side
    step_size = 1.0 / center
    for index_step in range(ITERS):
        if index_step > 0:
            factor = 0.5 if index_step == 1 else 0.25
            momentum = factor * (half_span * step_size) ** 2
            step_size = 1.0 / (center - momentum / step_size)
            search = residual + momentum * search
        solution = solution + step_size * search
        if index_step + 1 < ITERS:
            residual = residual - step_size * apply_fn(search)
    return solution


def solve_group(queries, key_rows, value_rows, grad_rows, cumulative, ridge, gram_state, memory):
    weights = decay_table(cumulative)
    scale = jnp.exp(cumulative)[:, None]
    trace_rows = scale[:, 0] * jnp.trace(gram_state) + product(weights, jnp.sum(key_rows * key_rows, axis=1))
    half_span = 0.5 * trace_rows[:, None]
    center = ridge + half_span

    def apply_fn(search):
        return ridge * search + scale * product(search, gram_state) + product(weights * product(search, key_rows.T), key_rows)

    solved = chebyshev(queries, apply_fn, center, half_span)
    output = scale * product(solved, memory.T) + product(weights * product(solved, key_rows.T), value_rows)
    pulled = scale * product(grad_rows, memory) + product(weights * product(grad_rows, value_rows.T), key_rows)
    query_rows = chebyshev(pulled, apply_fn, center, half_span)
    return output, query_rows


def local_states(key_rows, value_rows, cumulative):
    tail_weight = jnp.exp(cumulative[-1] - cumulative)[:, None]
    return product((key_rows * tail_weight).T, key_rows), product((value_rows * tail_weight).T, key_rows)


def run_head(item_set):
    queries, key_rows, value_rows, grad_rows, log_steps, ridge = item_set
    zero_state = jnp.zeros((queries.shape[-1], queries.shape[-1]), queries.dtype)

    def group_step(carried, pieces):
        gram_state, memory = carried
        group_query, group_key, group_value, group_grad, group_log = pieces
        cumulative = jnp.cumsum(group_log)
        output, query_rows = solve_group(group_query, group_key, group_value, group_grad, cumulative, ridge, gram_state, memory)
        gram_local, memory_local = local_states(group_key, group_value, cumulative)
        last_decay = jnp.exp(cumulative[-1])
        return (last_decay * gram_state + gram_local, last_decay * memory + memory_local), (output, query_rows)

    final_state, results = lax.scan(group_step, (zero_state, zero_state), (queries, key_rows, value_rows, grad_rows, log_steps))
    return results


def to_heads(array):
    shaped = array.reshape(BATCH_SEQUENCES, SEQUENCE_LENGTH, H, DH).transpose(0, 2, 1, 3)
    return shaped.reshape(BATCH_SEQUENCES * H, SEQUENCE_LENGTH // GROUP, GROUP, DH).astype(jnp.float32)


def from_heads(array):
    return array.reshape(BATCH_SEQUENCES, H, SEQUENCE_LENGTH, DH).transpose(0, 2, 1, 3).reshape(BATCH_SEQUENCES, SEQUENCE_LENGTH, H * DH)


def reference(tokens, w_query, keys, values, log_decay, regular, grad_out):
    flat_tokens = tokens.reshape(BATCH_SEQUENCES * SEQUENCE_LENGTH, D)
    queries = jnp.dot(flat_tokens, w_query, preferred_element_type=jnp.float32).astype(jnp.bfloat16)
    queries = lax.optimization_barrier(queries)
    ridge = jnp.broadcast_to(regular[None, :], (BATCH_SEQUENCES, H)).reshape(BATCH_SEQUENCES * H)
    log_steps = log_decay.reshape(BATCH_SEQUENCES * H, SEQUENCE_LENGTH // GROUP, GROUP)
    outputs, query_rows = lax.map(run_head, (to_heads(queries), to_heads(keys), to_heads(values), to_heads(grad_out), log_steps, ridge))
    mixed = from_heads(outputs).astype(jnp.bfloat16)
    grad_flat = from_heads(query_rows).astype(jnp.bfloat16).reshape(BATCH_SEQUENCES * SEQUENCE_LENGTH, H * DH)
    query_grad = lax.dot_general(grad_flat, flat_tokens, (((0,), (0,)), ((), ())), preferred_element_type=jnp.float32)
    return mixed, query_grad
```

```python
import functools

import jax
import jax.numpy as jnp
from jax import lax
from jax.experimental import pallas as pl
from jax.experimental.pallas import tpu as pltpu
from jax.sharding import PartitionSpec as P

F32 = jnp.float32
BF16 = jnp.bfloat16
MESH = pl.DeviceIdType.MESH

H = 8
C = 128
S = 4
ROWS = S * C
D = 2048
MSG = C + 8
ITERS = 4


def dot(a, b):
    return lax.dot_general(a, b, (((1,), (0,)), ((), ())), preferred_element_type=F32)


def dot_nt(a, b):
    return lax.dot_general(a, b, (((1,), (1,)), ((), ())), preferred_element_type=F32)


def dot_tn(a, b):
    return lax.dot_general(a, b, (((0,), (0,)), ((), ())), preferred_element_type=F32)


def kernel(
    tok_hbm, wq_hbm, k_hbm, v_hbm, ld_ref, reg_ref, g_hbm,
    mixed_hbm, qg_ref,
    tok, wq, kb, vb, gb, qb, mx,
    bs, el, wl, tl, ul, ll,
    loc, sib, tot, inbox, pre, pin, snd, st,
    gp, gin, zc, za, fin,
    load_sem, out_sem,
    sib_send, sib_recv, fw_send, fw_recv, bk_send, bk_recv, st_send, st_recv,
    gs_send, gs_recv, zc_send, zc_recv, za_send, za_recv, fin_send, fin_recv,
):
    dp = lax.axis_index("dp")
    seq = lax.axis_index("seq")
    core = lax.rem(seq, 2)
    other = 1 - core
    chip = lax.div(seq, 2)
    zpos = lax.div(chip, 2)
    ylo = lax.rem(chip, 2)
    twin = (dp, chip * 2 + other)

    def at_chip(c):
        return (dp, c * 2 + core)

    def at_z(z):
        return (dp, (z * 2 + ylo) * 2 + core)

    z_up = lax.rem(zpos + 1, 4)
    z_down = lax.rem(zpos + 3, 4)
    z_far = lax.rem(zpos + 2, 4)

    def remote(src, dst, send, recv, device):
        return pltpu.make_async_remote_copy(
            src_ref=src, dst_ref=dst, send_sem=send, recv_sem=recv, device_id=device, device_id_type=MESH
        )

    loads = [
        pltpu.make_async_copy(src, dst, load_sem.at[n])
        for n, (src, dst) in enumerate(
            ((k_hbm, kb), (v_hbm, vb), (wq_hbm, wq), (tok_hbm, tok), (g_hbm, gb))
        )
    ]
    for copy in loads:
        copy.start()

    barrier = pltpu.get_barrier_semaphore()
    pl.semaphore_signal(barrier, inc=1, device_id=twin, device_id_type=MESH)
    for n in range(1, 8):
        pl.semaphore_signal(barrier, inc=1, device_id=at_chip(lax.rem(chip + n, 8)), device_id_type=MESH)
    for n in range(1, 8):
        to = lax.rem(dp + n, 8)
        for y in range(2):
            pl.semaphore_signal(barrier, inc=1, device_id=(to, (zpos * 2 + y) * 2 + core), device_id_type=MESH)

    row_at = lax.broadcasted_iota(jnp.int32, (C, C), 0)
    col_at = lax.broadcasted_iota(jnp.int32, (C, C), 1)
    lower = row_at >= col_at
    eye = row_at == col_at

    def lanes(h):
        return pl.ds(pl.multiple_of(h * C, C), C)

    upper_ones = jnp.where(row_at <= col_at, 1.0, 0.0).astype(F32)
    for s in range(S):
        sums = lax.dot_general(
            ld_ref[:, s * C : (s + 1) * C], upper_ones, (((1,), (0,)), ((), ())),
            precision=lax.Precision.HIGHEST, preferred_element_type=F32,
        )
        for h in range(H):
            bs[h, s : s + 1, :] = sums[h : h + 1, :]

    loads[0].wait()
    loads[1].wait()

    def local_states(h, carry):
        m_sum = g_sum = None
        decay = None
        for s in range(S):
            rows = slice(s * C, (s + 1) * C)
            across = jnp.broadcast_to(bs[h, s : s + 1, :], (C, C))
            down = across.T
            e = jnp.exp(down)
            el[h, s] = e
            tail = jnp.exp(down[C - 1 : C, :] - down)
            k = kb[rows, lanes(h)]
            kt = (k.astype(F32) * tail).astype(BF16)
            vt = (vb[rows, lanes(h)].astype(F32) * tail).astype(BF16)
            m_new = dot_tn(vt, k)
            g_new = dot_tn(kt, k)
            ll[h, s, 0:C, :] = m_new
            ll[h, s, C : 2 * C, :] = g_new
            last = e[C - 1 : C, :]
            if s == 0:
                m_sum, g_sum, decay = m_new, g_new, last
            else:
                m_sum = last * m_sum + m_new
                g_sum = last * g_sum + g_new
                decay = decay * last
        tile = jnp.broadcast_to(decay, (8, C))
        loc[0, h, 0:C, :] = m_sum
        loc[0, h, C:MSG, :] = tile
        loc[1, h, 0:C, :] = g_sum
        loc[1, h, C:MSG, :] = tile
        return carry

    lax.fori_loop(0, H, local_states, 0)

    pl.semaphore_wait(barrier, 22)

    to_twin = remote(loc.at[other], sib, sib_send.at[0], sib_recv.at[0], twin)
    to_twin.start()

    loads[4].wait()

    def tables(h, carry):
        for s in range(S):
            rows = slice(s * C, (s + 1) * C)
            across = jnp.broadcast_to(bs[h, s : s + 1, :], (C, C))
            w = jnp.where(lower, jnp.exp(jnp.where(lower, across.T - across, 0.0)), 0.0)
            wl[h, s] = w
            k = kb[rows, lanes(h)]
            kf = k.astype(F32)
            square = jnp.broadcast_to(jnp.sum(kf * kf, axis=1, keepdims=True), (C, C))
            high = square.astype(BF16)
            low = (square - high.astype(F32)).astype(BF16)
            wb = w.astype(BF16)
            tl[h, s] = dot(jnp.concatenate([wb, wb], axis=1), jnp.concatenate([high, low], axis=0))
            ul[h, s] = (w * dot_nt(gb[rows, lanes(h)], vb[rows, lanes(h)])).astype(BF16)
        return carry

    lax.fori_loop(0, H // 2, tables, 0)

    to_twin.wait_recv()

    def total(h):
        mine_at = loc[core, h, C:MSG, :]
        sib_at = sib[h, C:MSG, :]
        first = core == 0
        by_mine = jnp.where(first, sib_at, 1.0)
        by_sib = jnp.where(first, 1.0, mine_at)
        tot[h, C:MSG, :] = mine_at * sib_at
        mine = loc[core, h, 0:C, :].reshape(C // 8, 8, C)
        theirs = sib[h, 0:C, :].reshape(C // 8, 8, C)
        tot[h, 0:C, :] = (by_mine[None] * mine + by_sib[None] * theirs).reshape(C, C)

    def forward(h):
        return remote(tot.at[h], inbox.at[chip], fw_send.at[h], fw_recv.at[chip], at_chip(h))

    def send_total(n, carry):
        h = lax.rem(chip + n, 8)
        total(h)
        forward(h).start()
        return carry

    lax.fori_loop(1, 8, send_total, 0)
    total(chip)
    inbox[chip] = tot[chip]

    lax.fori_loop(H // 2, H, tables, 0)

    loads[2].wait()
    loads[3].wait()
    for n in range(H // 2):
        block = dot(tok[...], wq[:, n * 2 * C : (n + 1) * 2 * C]).astype(BF16)
        qb[2 * n] = block[:, 0:C]
        qb[2 * n + 1] = block[:, C : 2 * C]

    def back(c):
        return remote(pre.at[c], pin.at[chip], bk_send.at[c], bk_recv.at[chip], at_chip(c))

    state = jnp.zeros((C // 8, 8, C), F32)
    for c in range(8):
        pre[c] = state.reshape(C, C)

        @pl.when(c != chip)
        def _():
            back(c).start()
            remote(tot.at[c], inbox.at[c], fw_send.at[c], fw_recv.at[c], at_chip(c)).wait_recv()

        state = inbox[c, C:MSG, :][None] * state + inbox[c, 0:C, :].reshape(C // 8, 8, C)
    pin[chip] = pre[chip]

    def hand_over(h):
        return remote(snd.at[h], st.at[core, h], st_send.at[h], st_recv.at[h], twin)

    def spread(n, carry):
        h = lax.rem(dp + 1 + n, 8)

        @pl.when(h != chip)
        def _():
            remote(pre.at[h], pin.at[h], bk_send.at[h], bk_recv.at[h], at_chip(h)).wait_recv()

        base = pin[h].reshape(C // 8, 8, C)
        mine_at = loc[core, h, C:MSG, :]
        sib_at = sib[h, C:MSG, :]
        mine = mine_at[None] * base + loc[core, h, 0:C, :].reshape(C // 8, 8, C)
        theirs = sib_at[None] * base + sib[h, 0:C, :].reshape(C // 8, 8, C)
        first = core == 0
        snd[h] = jnp.where(first, mine, base).reshape(C, C)
        st[core, h] = jnp.where(first, base, theirs).reshape(C, C)
        hand_over(h).start()
        return carry

    lax.fori_loop(0, H, spread, 0)

    def apply(pq, pg, e, w, state, k):
        p = jnp.concatenate([pq, pg], axis=0).astype(BF16)
        scores = dot_nt(p, k)
        left = jnp.concatenate(
            [
                jnp.concatenate([e * pq, e * pg], axis=0).astype(BF16),
                jnp.concatenate([w * scores[0:C], w * scores[C : 2 * C]], axis=0).astype(BF16),
            ],
            axis=1,
        )
        y = dot(left, jnp.concatenate([state, k], axis=0))
        return y[0:C], y[C : 2 * C]

    def solve(n):
        h = lax.rem(dp + 1 + n, 8)
        ridge = reg_ref[h]
        remote(snd.at[h], st.at[other, h], st_send.at[h], st_recv.at[h], twin).wait_recv()
        m, g = st[0, h], st[1, h]
        trace = jnp.sum(jnp.sum(jnp.where(eye, g, 0.0), axis=0, keepdims=True), axis=1, keepdims=True)
        trace = jnp.broadcast_to(trace, (1, C))
        each = []
        for s in range(S):
            rows = slice(s * C, (s + 1) * C)
            e, w = el[h, s], wl[h, s]
            spans = e * trace + tl[h, s]
            trace = spans[C - 1 : C, :]
            half = 0.5 * spans
            center = ridge + half
            square = half * half
            alpha = 1.0 / center
            alphas, betas = [alpha], [None]
            for step in range(1, ITERS):
                factor = 0.5 if step == 1 else 0.25
                betas.append(factor * (half * alpha) * (half * alpha))
                alpha = 1.0 / (center - factor * square * alpha)
                alphas.append(alpha)
            each.append(dict(rows=rows, e=e, w=w, m=m.astype(BF16), g=g.astype(BF16), a=alphas, b=betas))
            if s + 1 < S:
                last = e[C - 1 : C, :]
                m = last * m + ll[h, s, 0:C, :]
                g = last * g + ll[h, s, C : 2 * C, :]
        for s, t in enumerate(each):
            k = kb[t["rows"], lanes(h)]
            grad = gb[t["rows"], lanes(h)].astype(F32)
            left = jnp.concatenate([(t["e"] * grad).astype(BF16), ul[h, s]], axis=1)
            rg = dot(left, jnp.concatenate([t["m"], k], axis=0))
            rq = qb[h, t["rows"], :].astype(F32)
            t.update(k=k, rq=rq, rg=rg, pq=rq, pg=rg, xq=t["a"][0] * rq, xg=t["a"][0] * rg)
        for step in range(1, ITERS):
            for t in each:
                yq, yg = apply(t["pq"], t["pg"], t["e"], t["w"], t["g"], t["k"])
                before, now, beta = t["a"][step - 1], t["a"][step], t["b"][step]
                for i, y in (("q", yq), ("g", yg)):
                    res = t["r" + i] - before * (ridge * t["p" + i] + y)
                    p = res + beta * t["p" + i]
                    t["r" + i], t["p" + i] = res, p
                    t["x" + i] = t["x" + i] + now * p
        solved = []
        for s, t in enumerate(each):
            scores = dot_nt(t["xq"].astype(BF16), t["k"])
            y = dot_nt((t["e"] * t["xq"]).astype(BF16), t["m"])
            y = y + dot((t["w"] * scores).astype(BF16), vb[t["rows"], lanes(h)])
            mx[t["rows"], lanes(h)] = y.astype(BF16)
            solved.append(t["xg"].T.astype(BF16))
        left = jnp.concatenate(solved, axis=1)
        for c in range(8):
            part = dot(left, tok[:, c * 2 * C : (c + 1) * 2 * C])
            gp[n, 0, c] = part[:, 0:C]
            gp[n, 1, c] = part[:, C : 2 * C]

    def out_copy(n):
        h = lax.rem(dp + 1 + n, 8)
        return pltpu.make_async_copy(mx.at[:, lanes(h)], mixed_hbm.at[:, lanes(h)], out_sem.at[n])

    def to_core(n):
        return remote(gp.at[n, other], gin.at[n], gs_send.at[n], gs_recv.at[n], twin)

    def far_up(n):
        return remote(gp.at[n, core, z_far * 2], zc.at[n, 0], zc_send.at[n, 0], zc_recv.at[n, 0], at_z(z_up))

    def far_down(n):
        return remote(gp.at[n, core, z_far * 2 + 1], zc.at[n, 1], zc_send.at[n, 1], zc_recv.at[n, 1], at_z(z_down))

    def near_up(n):
        return remote(gp.at[n, core, pl.ds(z_up * 2, 2)], za.at[n, 0], za_send.at[n, 0], za_recv.at[n, 0], at_z(z_up))

    def near_down(n):
        return remote(
            gp.at[n, core, pl.ds(z_down * 2, 2)], za.at[n, 1], za_send.at[n, 1], za_recv.at[n, 1], at_z(z_down)
        )

    def finish(n, y):
        h = lax.rem(dp + 1 + n, 8)
        return remote(
            gp.at[n, core, zpos * 2 + y], fin.at[dp * 2 + ylo], fin_send.at[n, y], fin_recv.at[dp * 2 + ylo],
            (h, (zpos * 2 + y) * 2 + core),
        )

    def turn(i, carry):
        @pl.when(i < H)
        def _():
            solve(i)
            to_core(i).start()
            out_copy(i).start()

        @pl.when((i >= 1) & (i < H + 1))
        def _():
            n = i - 1
            to_core(n).wait_recv()
            gp[n, core] = gp[n, core] + gin[n]
            far_up(n).start()
            far_down(n).start()

        @pl.when((i >= 2) & (i < H + 2))
        def _():
            n = i - 2
            far_up(n).wait_recv()
            far_down(n).wait_recv()
            gp[n, core, z_up * 2] = gp[n, core, z_up * 2] + zc[n, 0]
            gp[n, core, z_down * 2 + 1] = gp[n, core, z_down * 2 + 1] + zc[n, 1]
            near_up(n).start()
            near_down(n).start()

        @pl.when((i >= 3) & (i < H + 3))
        def _():
            n = i - 3
            near_up(n).wait_recv()
            near_down(n).wait_recv()
            for y in range(2):
                gp[n, core, zpos * 2 + y] = gp[n, core, zpos * 2 + y] + za[n, 0, y] + za[n, 1, y]

                @pl.when((n < H - 1) | (ylo != y))
                def _():
                    finish(n, y).start()

                @pl.when((n == H - 1) & (ylo == y))
                def _():
                    fin[dp * 2 + y] = gp[n, core, zpos * 2 + y]

        return carry

    lax.fori_loop(0, H + 3, turn, 0)

    acc = None
    for source in range(16):

        @pl.when(dp * 2 + ylo != source)
        def _():
            remote(
                gp.at[0, core, 0], fin.at[source], fin_send.at[0, 0], fin_recv.at[source], twin
            ).wait_recv()

        acc = fin[source] if acc is None else acc + fin[source]
    qg_ref[...] = acc

    to_twin.wait_send()

    def drain(n, carry):
        @pl.when(n != chip)
        def _():
            forward(n).wait_send()
            back(n).wait_send()

        hand_over(n).wait_send()
        out_copy(n).wait()
        to_core(n).wait_send()
        far_up(n).wait_send()
        far_down(n).wait_send()
        near_up(n).wait_send()
        near_down(n).wait_send()
        for y in range(2):

            @pl.when((n < H - 1) | (ylo != y))
            def _():
                finish(n, y).wait_send()

        return carry

    lax.fori_loop(0, H, drain, 0)


def per_device(tokens, w_query, keys, values, log_decay, regular, grad_out):
    dma = pltpu.SemaphoreType.DMA
    hbm = pl.BlockSpec(memory_space=pl.ANY)
    vmem = pl.BlockSpec(memory_space=pltpu.VMEM)
    smem = pl.BlockSpec(memory_space=pltpu.SMEM)
    mixed, query_grad = pl.pallas_call(
        kernel,
        out_shape=(
            jax.ShapeDtypeStruct((ROWS, H * C), BF16),
            jax.ShapeDtypeStruct((C, C), F32),
        ),
        in_specs=[hbm, hbm, hbm, hbm, vmem, smem, hbm],
        out_specs=(hbm, vmem),
        scratch_shapes=[
            pltpu.VMEM((ROWS, D), BF16),
            pltpu.VMEM((D, H * C), BF16),
            pltpu.VMEM((ROWS, H * C), BF16),
            pltpu.VMEM((ROWS, H * C), BF16),
            pltpu.VMEM((ROWS, H * C), BF16),
            pltpu.VMEM((H, ROWS, C), BF16),
            pltpu.VMEM((ROWS, H * C), BF16),
            pltpu.VMEM((H, S, C), F32),
            pltpu.VMEM((H, S, C, C), F32),
            pltpu.VMEM((H, S, C, C), F32),
            pltpu.VMEM((H, S, C, C), F32),
            pltpu.VMEM((H, S, C, C), BF16),
            pltpu.VMEM((H, S, 2 * C, C), F32),
            pltpu.VMEM((2, H, MSG, C), F32),
            pltpu.VMEM((H, MSG, C), F32),
            pltpu.VMEM((H, MSG, C), F32),
            pltpu.VMEM((H, MSG, C), F32),
            pltpu.VMEM((H, C, C), F32),
            pltpu.VMEM((H, C, C), F32),
            pltpu.VMEM((H, C, C), F32),
            pltpu.VMEM((2, H, C, C), F32),
            pltpu.VMEM((H, 2, 8, C, C), F32),
            pltpu.VMEM((H, 8, C, C), F32),
            pltpu.VMEM((H, 2, C, C), F32),
            pltpu.VMEM((H, 2, 2, C, C), F32),
            pltpu.VMEM((16, C, C), F32),
            dma((5,)),
            dma((H,)),
            dma((1,)),
            dma((1,)),
            dma((H,)),
            dma((H,)),
            dma((H,)),
            dma((H,)),
            dma((H,)),
            dma((H,)),
            dma((H,)),
            dma((H,)),
            dma((H, 2)),
            dma((H, 2)),
            dma((H, 2)),
            dma((H, 2)),
            dma((H, 2)),
            dma((16,)),
        ],
        compiler_params=pltpu.CompilerParams(
            collective_id=0, has_side_effects=True, vmem_limit_bytes=60 * 2**20
        ),
    )(
        tokens.reshape(ROWS, D),
        w_query,
        keys.reshape(ROWS, H * C),
        values.reshape(ROWS, H * C),
        log_decay.reshape(H, ROWS),
        regular,
        grad_out.reshape(ROWS, H * C),
    )
    return mixed.reshape(1, ROWS, H * C), query_grad


def solution(mesh):
    in_specs = (
        P("dp", "seq", None),
        P(),
        P("dp", "seq", None),
        P("dp", "seq", None),
        P("dp", None, "seq"),
        P(),
        P("dp", "seq", None),
    )
    out_specs = (P("dp", "seq", None), P("dp", "seq"))
    return jax.shard_map(
        per_device, mesh=mesh, in_specs=in_specs, out_specs=out_specs, check_vma=False
    )
```

```python
import functools

import jax
import jax.numpy as jnp
from jax import lax
from jax.experimental import pallas as pl
from jax.experimental.pallas import tpu as pltpu
from jax.sharding import PartitionSpec as P

F32 = jnp.float32
BF16 = jnp.bfloat16
MESH = pl.DeviceIdType.MESH

H = 8
C = 128
S = 4
ROWS = S * C
D = 2048
MSG = C + 8
ITERS = 4


def dot(a, b):
    return lax.dot_general(a, b, (((1,), (0,)), ((), ())), preferred_element_type=F32)


def dot_nt(a, b):
    return lax.dot_general(a, b, (((1,), (1,)), ((), ())), preferred_element_type=F32)


def dot_tn(a, b):
    return lax.dot_general(a, b, (((0,), (0,)), ((), ())), preferred_element_type=F32)


def kernel(
    tok_hbm, wq_hbm, k_hbm, v_hbm, ld_ref, reg_ref, g_hbm,
    mixed_hbm, qg_ref,
    tok, wq, kb, vb, gb, qb, mx,
    bs, el, wl, tl, ul, ll,
    loc, sib, tot, inbox, pre, pin, snd, st,
    gp, gin, zc, za, ya, fin,
    load_sem, out_sem,
    sib_send, sib_recv, fw_send, fw_recv, bk_send, bk_recv, st_send, st_recv,
    gs_send, gs_recv, zc_send, zc_recv, za_send, za_recv, fin_send, fin_recv,
):
    dp = lax.axis_index("dp")
    seq = lax.axis_index("seq")
    core = lax.rem(seq, 2)
    other = 1 - core
    chip = lax.div(seq, 2)
    zpos = lax.div(chip, 2)
    ylo = lax.rem(chip, 2)
    twin = (dp, chip * 2 + other)

    def at_chip(c):
        return (dp, c * 2 + core)

    def at_z(z):
        return (dp, (z * 2 + ylo) * 2 + core)

    z_up = lax.rem(zpos + 1, 4)
    z_down = lax.rem(zpos + 3, 4)
    z_far = lax.rem(zpos + 2, 4)

    def remote(src, dst, send, recv, device):
        return pltpu.make_async_remote_copy(
            src_ref=src, dst_ref=dst, send_sem=send, recv_sem=recv, device_id=device, device_id_type=MESH
        )

    loads = [
        pltpu.make_async_copy(src, dst, load_sem.at[n])
        for n, (src, dst) in enumerate(
            ((k_hbm, kb), (v_hbm, vb), (wq_hbm, wq), (tok_hbm, tok), (g_hbm, gb))
        )
    ]
    for copy in loads:
        copy.start()

    barrier = pltpu.get_barrier_semaphore()
    pl.semaphore_signal(barrier, inc=1, device_id=twin, device_id_type=MESH)
    for n in range(1, 8):
        pl.semaphore_signal(barrier, inc=1, device_id=at_chip(lax.rem(chip + n, 8)), device_id_type=MESH)
    near_same = (dp, (zpos * 2 + 1 - ylo) * 2 + core)
    near_other = (dp + 1 - 2 * lax.rem(dp, 2), (zpos * 2 + 1 - ylo) * 2 + core)

    def greet(device):
        pl.semaphore_signal(barrier, inc=1, device_id=device, device_id_type=MESH)

    @pl.when(core == 0)
    def _():
        for n in range(1, 8):
            for y in range(2):
                greet((lax.rem(dp + n, 8), (zpos * 2 + y) * 2))

    @pl.when(core == 1)
    def _():
        greet(near_other)
        for n in range(1, 4):
            for z in range(4):
                greet((lax.rem(dp + 2 * n, 8), (z * 2 + ylo) * 2 + 1))

    row_at = lax.broadcasted_iota(jnp.int32, (C, C), 0)
    col_at = lax.broadcasted_iota(jnp.int32, (C, C), 1)
    lower = row_at >= col_at
    eye = row_at == col_at

    xpos = lax.div(dp, 2)
    yhi = lax.rem(dp, 2)

    def head_at(n):
        return 2 * lax.rem(xpos + 1 + lax.div(n, 2), 4) + lax.rem(yhi + 1 + n, 2)

    def lanes(h):
        return pl.ds(pl.multiple_of(h * C, C), C)

    upper_ones = jnp.where(row_at <= col_at, 1.0, 0.0).astype(F32)
    for s in range(S):
        sums = lax.dot_general(
            ld_ref[:, s * C : (s + 1) * C], upper_ones, (((1,), (0,)), ((), ())),
            precision=lax.Precision.HIGHEST, preferred_element_type=F32,
        )
        for h in range(H):
            bs[h, s : s + 1, :] = sums[h : h + 1, :]

    loads[0].wait()
    loads[1].wait()

    def local_states(h, carry):
        m_sum = g_sum = None
        decay = None
        for s in range(S):
            rows = slice(s * C, (s + 1) * C)
            across = jnp.broadcast_to(bs[h, s : s + 1, :], (C, C))
            down = across.T
            e = jnp.exp(down)
            el[h, s] = e
            tail = jnp.exp(down[C - 1 : C, :] - down)
            k = kb[rows, lanes(h)]
            kt = (k.astype(F32) * tail).astype(BF16)
            vt = (vb[rows, lanes(h)].astype(F32) * tail).astype(BF16)
            m_new = dot_tn(vt, k)
            g_new = dot_tn(kt, k)
            ll[h, s, 0:C, :] = m_new
            ll[h, s, C : 2 * C, :] = g_new
            last = e[C - 1 : C, :]
            if s == 0:
                m_sum, g_sum, decay = m_new, g_new, last
            else:
                m_sum = last * m_sum + m_new
                g_sum = last * g_sum + g_new
                decay = decay * last
        tile = jnp.broadcast_to(decay, (8, C))
        loc[0, h, 0:C, :] = m_sum
        loc[0, h, C:MSG, :] = tile
        loc[1, h, 0:C, :] = g_sum
        loc[1, h, C:MSG, :] = tile
        return carry

    lax.fori_loop(0, H, local_states, 0)

    pl.semaphore_wait(barrier, jnp.where(core == 0, 22, 21))

    to_twin = remote(loc.at[other], sib, sib_send.at[0], sib_recv.at[0], twin)
    to_twin.start()

    loads[4].wait()

    def tables(h, carry):
        for s in range(S):
            rows = slice(s * C, (s + 1) * C)
            across = jnp.broadcast_to(bs[h, s : s + 1, :], (C, C))
            w = jnp.where(lower, jnp.exp(jnp.where(lower, across.T - across, 0.0)), 0.0)
            wl[h, s] = w
            k = kb[rows, lanes(h)]
            kf = k.astype(F32)
            square = jnp.broadcast_to(jnp.sum(kf * kf, axis=1, keepdims=True), (C, C))
            high = square.astype(BF16)
            low = (square - high.astype(F32)).astype(BF16)
            wb = w.astype(BF16)
            tl[h, s] = dot(jnp.concatenate([wb, wb], axis=1), jnp.concatenate([high, low], axis=0))
            ul[h, s] = (w * dot_nt(gb[rows, lanes(h)], vb[rows, lanes(h)])).astype(BF16)
        return carry

    lax.fori_loop(0, H // 2, tables, 0)

    to_twin.wait_recv()

    def total(h):
        mine_at = loc[core, h, C:MSG, :]
        sib_at = sib[h, C:MSG, :]
        first = core == 0
        by_mine = jnp.where(first, sib_at, 1.0)
        by_sib = jnp.where(first, 1.0, mine_at)
        tot[h, C:MSG, :] = mine_at * sib_at
        mine = loc[core, h, 0:C, :].reshape(C // 8, 8, C)
        theirs = sib[h, 0:C, :].reshape(C // 8, 8, C)
        tot[h, 0:C, :] = (by_mine[None] * mine + by_sib[None] * theirs).reshape(C, C)

    def forward(h):
        return remote(tot.at[h], inbox.at[chip], fw_send.at[h], fw_recv.at[chip], at_chip(h))

    def send_total(n, carry):
        h = lax.rem(chip + n, 8)
        total(h)
        forward(h).start()
        return carry

    lax.fori_loop(1, 8, send_total, 0)
    total(chip)
    inbox[chip] = tot[chip]

    lax.fori_loop(H // 2, H, tables, 0)

    loads[2].wait()
    loads[3].wait()
    for n in range(H // 2):
        block = dot(tok[...], wq[:, n * 2 * C : (n + 1) * 2 * C]).astype(BF16)
        qb[2 * n] = block[:, 0:C]
        qb[2 * n + 1] = block[:, C : 2 * C]

    def back(c):
        return remote(pre.at[c], pin.at[chip], bk_send.at[c], bk_recv.at[chip], at_chip(c))

    state = jnp.zeros((C // 8, 8, C), F32)
    for c in range(8):
        pre[c] = state.reshape(C, C)

        @pl.when(c != chip)
        def _():
            back(c).start()
            remote(tot.at[c], inbox.at[c], fw_send.at[c], fw_recv.at[c], at_chip(c)).wait_recv()

        state = inbox[c, C:MSG, :][None] * state + inbox[c, 0:C, :].reshape(C // 8, 8, C)
    pin[chip] = pre[chip]

    def hand_over(h):
        return remote(snd.at[h], st.at[core, h], st_send.at[h], st_recv.at[h], twin)

    def spread(n, carry):
        h = head_at(n)

        @pl.when(h != chip)
        def _():
            remote(pre.at[h], pin.at[h], bk_send.at[h], bk_recv.at[h], at_chip(h)).wait_recv()

        base = pin[h].reshape(C // 8, 8, C)
        mine_at = loc[core, h, C:MSG, :]
        sib_at = sib[h, C:MSG, :]
        mine = mine_at[None] * base + loc[core, h, 0:C, :].reshape(C // 8, 8, C)
        theirs = sib_at[None] * base + sib[h, 0:C, :].reshape(C // 8, 8, C)
        first = core == 0
        snd[h] = jnp.where(first, mine, base).reshape(C, C)
        st[core, h] = jnp.where(first, base, theirs).reshape(C, C)
        hand_over(h).start()
        return carry

    lax.fori_loop(0, H, spread, 0)

    def apply(pq, pg, e, w, state, k):
        p = jnp.concatenate([pq, pg], axis=0).astype(BF16)
        scores = dot_nt(p, k)
        left = jnp.concatenate(
            [
                jnp.concatenate([e * pq, e * pg], axis=0).astype(BF16),
                jnp.concatenate([w * scores[0:C], w * scores[C : 2 * C]], axis=0).astype(BF16),
            ],
            axis=1,
        )
        y = dot(left, jnp.concatenate([state, k], axis=0))
        return y[0:C], y[C : 2 * C]

    def solve(n):
        h = head_at(n)
        ridge = reg_ref[h]
        remote(snd.at[h], st.at[other, h], st_send.at[h], st_recv.at[h], twin).wait_recv()
        m, g = st[0, h], st[1, h]
        trace = jnp.sum(jnp.sum(jnp.where(eye, g, 0.0), axis=0, keepdims=True), axis=1, keepdims=True)
        trace = jnp.broadcast_to(trace, (1, C))
        each = []
        for s in range(S):
            rows = slice(s * C, (s + 1) * C)
            e, w = el[h, s], wl[h, s]
            spans = e * trace + tl[h, s]
            trace = spans[C - 1 : C, :]
            half = 0.5 * spans
            center = ridge + half
            square = half * half
            alpha = 1.0 / center
            alphas, betas = [alpha], [None]
            for step in range(1, ITERS):
                factor = 0.5 if step == 1 else 0.25
                betas.append(factor * (half * alpha) * (half * alpha))
                alpha = 1.0 / (center - factor * square * alpha)
                alphas.append(alpha)
            each.append(dict(rows=rows, e=e, w=w, m=m.astype(BF16), g=g.astype(BF16), a=alphas, b=betas))
            if s + 1 < S:
                last = e[C - 1 : C, :]
                m = last * m + ll[h, s, 0:C, :]
                g = last * g + ll[h, s, C : 2 * C, :]
        for s, t in enumerate(each):
            k = kb[t["rows"], lanes(h)]
            grad = gb[t["rows"], lanes(h)].astype(F32)
            left = jnp.concatenate([(t["e"] * grad).astype(BF16), ul[h, s]], axis=1)
            rg = dot(left, jnp.concatenate([t["m"], k], axis=0))
            rq = qb[h, t["rows"], :].astype(F32)
            t.update(k=k, rq=rq, rg=rg, pq=rq, pg=rg, xq=t["a"][0] * rq, xg=t["a"][0] * rg)
        for step in range(1, ITERS):
            for t in each:
                yq, yg = apply(t["pq"], t["pg"], t["e"], t["w"], t["g"], t["k"])
                before, now, beta = t["a"][step - 1], t["a"][step], t["b"][step]
                for i, y in (("q", yq), ("g", yg)):
                    res = t["r" + i] - before * (ridge * t["p" + i] + y)
                    p = res + beta * t["p" + i]
                    t["r" + i], t["p" + i] = res, p
                    t["x" + i] = t["x" + i] + now * p
        solved = []
        for s, t in enumerate(each):
            scores = dot_nt(t["xq"].astype(BF16), t["k"])
            y = dot_nt((t["e"] * t["xq"]).astype(BF16), t["m"])
            y = y + dot((t["w"] * scores).astype(BF16), vb[t["rows"], lanes(h)])
            mx[t["rows"], lanes(h)] = y.astype(BF16)
            solved.append(t["xg"].T.astype(BF16))
        left = jnp.concatenate(solved, axis=1)
        for c in range(8):
            part = dot(left, tok[:, c * 2 * C : (c + 1) * 2 * C])
            gp[n, 0, c // 2, c % 2] = part[:, 0:C]
            gp[n, 1, c // 2, c % 2] = part[:, C : 2 * C]

    def out_copy(n):
        h = head_at(n)
        return pltpu.make_async_copy(mx.at[:, lanes(h)], mixed_hbm.at[:, lanes(h)], out_sem.at[n])

    def to_core(n):
        return remote(gp.at[n, other], gin.at[n], gs_send.at[n], gs_recv.at[n], twin)

    def far_up(n):
        return remote(gp.at[n, 0, z_far, 0], zc.at[n, 0], zc_send.at[n, 0], zc_recv.at[n, 0], at_z(z_up))

    def far_down(n):
        return remote(gp.at[n, 0, z_far, 1], zc.at[n, 1], zc_send.at[n, 1], zc_recv.at[n, 1], at_z(z_down))

    def near_up(n):
        return remote(gp.at[n, 0, z_up], za.at[n, 0], za_send.at[n, 0], za_recv.at[n, 0], at_z(z_up))

    def near_down(n):
        return remote(gp.at[n, 0, z_down], za.at[n, 1], za_send.at[n, 1], za_recv.at[n, 1], at_z(z_down))

    def finish_z(n, y):
        at = dp * 2 + ylo
        return remote(
            gp.at[n, 0, zpos, y], fin.at[at], fin_send.at[n, y], fin_recv.at[at], (head_at(n), (zpos * 2 + y) * 2)
        )

    def far_same(n):
        return remote(
            gp.at[n, 1, 0:2, ylo], zc.at[n], zc_send.at[n, 0], zc_recv.at[n, 0], near_same
        )

    def far_other(n):
        return remote(
            gp.at[n, 1, 2:4, ylo], zc.at[n + 1], zc_send.at[n, 1], zc_recv.at[n, 1], near_other
        )

    def send_other(n):
        return remote(gp.at[n, 1, :, 1 - ylo], ya.at[n], za_send.at[n, 0], za_recv.at[n, 0], near_other)

    def send_same(n):
        return remote(gp.at[n, 1, :, 1 - ylo], ya.at[n], za_send.at[n, 0], za_recv.at[n, 0], near_same)

    def finish_y(n, z):
        at = xpos * 4 + zpos
        return remote(
            gp.at[n, 1, z, ylo], fin.at[at], fin_send.at[n, z], fin_recv.at[at], (head_at(n), (z * 2 + ylo) * 2 + 1)
        )

    def odd(n):
        return lax.rem(n, 2) == 1

    def even(n):
        return lax.rem(n, 2) == 0

    def turn(i, carry):
        @pl.when(i < H)
        def _():
            solve(i)
            to_core(i).start()
            out_copy(i).start()

        n1, n2, n3 = i - 1, i - 2, i - 3
        in1 = (i >= 1) & (i < H + 1)
        in2 = (i >= 2) & (i < H + 2)
        in3 = (i >= 3) & (i < H + 3)

        @pl.when(in1)
        def _():
            to_core(n1).wait_recv()
            gp[n1, core] = gp[n1, core] + gin[n1]

        @pl.when(in1 & (core == 0))
        def _():
            far_up(n1).start()
            far_down(n1).start()

        @pl.when(in2 & (core == 0))
        def _():
            far_up(n2).wait_recv()
            far_down(n2).wait_recv()
            gp[n2, 0, z_up, 0] = gp[n2, 0, z_up, 0] + zc[n2, 0]
            gp[n2, 0, z_down, 1] = gp[n2, 0, z_down, 1] + zc[n2, 1]
            near_up(n2).start()
            near_down(n2).start()

        @pl.when(in3 & (core == 0))
        def _():
            near_up(n3).wait_recv()
            near_down(n3).wait_recv()
            for y in range(2):
                gp[n3, 0, zpos, y] = gp[n3, 0, zpos, y] + za[n3, 0, y] + za[n3, 1, y]

                @pl.when((n3 < H - 1) | (ylo != y))
                def _():
                    finish_z(n3, y).start()

                @pl.when((n3 == H - 1) & (ylo == y))
                def _():
                    fin[dp * 2 + y] = gp[n3, 0, zpos, y]

        @pl.when(in1 & (core == 1) & even(n1))
        def _():
            far_same(n1).start()
            far_other(n1).start()

        @pl.when(in1 & (core == 1) & odd(n1))
        def _():
            far_other(n1 - 1).wait_recv()
            gp[n1, 1, 2:4, 1 - ylo] = gp[n1, 1, 2:4, 1 - ylo] + zc[n1]
            send_same(n1).start()

        @pl.when(in2 & (core == 1) & even(n2))
        def _():
            far_same(n2).wait_recv()
            gp[n2, 1, 0:2, 1 - ylo] = gp[n2, 1, 0:2, 1 - ylo] + zc[n2]
            send_other(n2).start()

        @pl.when(in3 & (core == 1) & odd(n3))
        def _():
            send_other(n3 - 1).wait_recv()
            send_same(n3).wait_recv()
            for z in range(4):
                gp[n3, 1, z, ylo] = gp[n3, 1, z, ylo] + ya[n3 - 1, z] + ya[n3, z]

                @pl.when((n3 < H - 1) | (zpos != z))
                def _():
                    finish_y(n3, z).start()

                @pl.when((n3 == H - 1) & (zpos == z))
                def _():
                    fin[xpos * 4 + z] = gp[n3, 1, z, ylo]

        return carry

    lax.fori_loop(0, H + 3, turn, 0)

    acc = None
    own = jnp.where(core == 0, dp * 2 + ylo, xpos * 4 + zpos)
    for source in range(16):

        @pl.when(own != source)
        def _():
            remote(gp.at[0, 0, 0, 0], fin.at[source], fin_send.at[0, 0], fin_recv.at[source], twin).wait_recv()

        acc = fin[source] if acc is None else acc + fin[source]
    qg_ref[...] = acc

    to_twin.wait_send()

    def drain(n, carry):
        @pl.when(n != chip)
        def _():
            forward(n).wait_send()
            back(n).wait_send()

        hand_over(n).wait_send()
        out_copy(n).wait()
        to_core(n).wait_send()

        @pl.when(core == 0)
        def _():
            far_up(n).wait_send()
            far_down(n).wait_send()
            near_up(n).wait_send()
            near_down(n).wait_send()
            for y in range(2):

                @pl.when((n < H - 1) | (ylo != y))
                def _():
                    finish_z(n, y).wait_send()

        @pl.when((core == 1) & even(n))
        def _():
            far_same(n).wait_send()
            far_other(n).wait_send()
            send_other(n).wait_send()

        @pl.when((core == 1) & odd(n))
        def _():
            send_same(n).wait_send()
            for z in range(4):

                @pl.when((n < H - 1) | (zpos != z))
                def _():
                    finish_y(n, z).wait_send()

        return carry

    lax.fori_loop(0, H, drain, 0)


def per_device(tokens, w_query, keys, values, log_decay, regular, grad_out):
    dma = pltpu.SemaphoreType.DMA
    hbm = pl.BlockSpec(memory_space=pl.ANY)
    vmem = pl.BlockSpec(memory_space=pltpu.VMEM)
    smem = pl.BlockSpec(memory_space=pltpu.SMEM)
    mixed, query_grad = pl.pallas_call(
        kernel,
        out_shape=(
            jax.ShapeDtypeStruct((ROWS, H * C), BF16),
            jax.ShapeDtypeStruct((C, C), F32),
        ),
        in_specs=[hbm, hbm, hbm, hbm, vmem, smem, hbm],
        out_specs=(hbm, vmem),
        scratch_shapes=[
            pltpu.VMEM((ROWS, D), BF16),
            pltpu.VMEM((D, H * C), BF16),
            pltpu.VMEM((ROWS, H * C), BF16),
            pltpu.VMEM((ROWS, H * C), BF16),
            pltpu.VMEM((ROWS, H * C), BF16),
            pltpu.VMEM((H, ROWS, C), BF16),
            pltpu.VMEM((ROWS, H * C), BF16),
            pltpu.VMEM((H, S, C), F32),
            pltpu.VMEM((H, S, C, C), F32),
            pltpu.VMEM((H, S, C, C), F32),
            pltpu.VMEM((H, S, C, C), F32),
            pltpu.VMEM((H, S, C, C), BF16),
            pltpu.VMEM((H, S, 2 * C, C), F32),
            pltpu.VMEM((2, H, MSG, C), F32),
            pltpu.VMEM((H, MSG, C), F32),
            pltpu.VMEM((H, MSG, C), F32),
            pltpu.VMEM((H, MSG, C), F32),
            pltpu.VMEM((H, C, C), F32),
            pltpu.VMEM((H, C, C), F32),
            pltpu.VMEM((H, C, C), F32),
            pltpu.VMEM((2, H, C, C), F32),
            pltpu.VMEM((H, 2, 4, 2, C, C), F32),
            pltpu.VMEM((H, 4, 2, C, C), F32),
            pltpu.VMEM((H, 2, C, C), F32),
            pltpu.VMEM((H, 2, 2, C, C), F32),
            pltpu.VMEM((H, 4, C, C), F32),
            pltpu.VMEM((16, C, C), F32),
            dma((5,)),
            dma((H,)),
            dma((1,)),
            dma((1,)),
            dma((H,)),
            dma((H,)),
            dma((H,)),
            dma((H,)),
            dma((H,)),
            dma((H,)),
            dma((H,)),
            dma((H,)),
            dma((H, 2)),
            dma((H, 2)),
            dma((H, 2)),
            dma((H, 2)),
            dma((H, 4)),
            dma((16,)),
        ],
        compiler_params=pltpu.CompilerParams(
            collective_id=0, has_side_effects=True, vmem_limit_bytes=60 * 2**20
        ),
    )(
        tokens.reshape(ROWS, D),
        w_query,
        keys.reshape(ROWS, H * C),
        values.reshape(ROWS, H * C),
        log_decay.reshape(H, ROWS),
        regular,
        grad_out.reshape(ROWS, H * C),
    )
    return mixed.reshape(1, ROWS, H * C), query_grad


def solution(mesh):
    in_specs = (
        P("dp", "seq", None),
        P(),
        P("dp", "seq", None),
        P("dp", "seq", None),
        P("dp", None, "seq"),
        P(),
        P("dp", "seq", None),
    )
    out_specs = (P("dp", "seq", None), P("dp", "seq"))
    return jax.shard_map(
        per_device, mesh=mesh, in_specs=in_specs, out_specs=out_specs, check_vma=False
    )
```

```python
import functools

import jax
import jax.numpy as jnp
from jax import lax
from jax.experimental import pallas as pl
from jax.experimental.pallas import tpu as pltpu
from jax.sharding import PartitionSpec as P

F32 = jnp.float32
BF16 = jnp.bfloat16
MESH = pl.DeviceIdType.MESH

H = 8
C = 128
S = 4
ROWS = S * C
D = 2048
MSG = C + 8
HALF = C // 2
ITERS = 4
FAR, SAME, NEAR = 3, 2, 5


def dot(a, b):
    return lax.dot_general(a, b, (((1,), (0,)), ((), ())), preferred_element_type=F32)


def dot_nt(a, b):
    return lax.dot_general(a, b, (((1,), (1,)), ((), ())), preferred_element_type=F32)


def dot_tn(a, b):
    return lax.dot_general(a, b, (((0,), (0,)), ((), ())), preferred_element_type=F32)


def kernel(
    tok_hbm, wq_hbm, k_hbm, v_hbm, ld_ref, reg_ref, g_hbm,
    mixed_hbm, qg_ref,
    tok, wq, kb, vb, gb, qb, mx,
    bs, el, wl, tl, ul, ll,
    loc, sib, tot, inbox, pre, pin, snd, st,
    gp, gin, zc, za, ya, fin,
    load_sem, out_sem,
    sib_send, sib_recv, fw_send, fw_recv, bk_send, bk_recv, st_send, st_recv,
    gs_send, gs_recv, zc_send, zc_recv, za_send, za_recv, fin_send, fin_recv,
):
    dp = lax.axis_index("dp")
    seq = lax.axis_index("seq")
    core = lax.rem(seq, 2)
    other = 1 - core
    chip = lax.div(seq, 2)
    zpos = lax.div(chip, 2)
    ylo = lax.rem(chip, 2)
    twin = (dp, chip * 2 + other)

    def at_chip(c):
        return (dp, c * 2 + core)

    def at_z(z):
        return (dp, (z * 2 + ylo) * 2 + core)

    z_up = lax.rem(zpos + 1, 4)
    z_down = lax.rem(zpos + 3, 4)
    z_far = lax.rem(zpos + 2, 4)

    def remote(src, dst, send, recv, device):
        return pltpu.make_async_remote_copy(
            src_ref=src, dst_ref=dst, send_sem=send, recv_sem=recv, device_id=device, device_id_type=MESH
        )

    loads = [
        pltpu.make_async_copy(src, dst, load_sem.at[n])
        for n, (src, dst) in enumerate(
            ((k_hbm, kb), (v_hbm, vb), (wq_hbm, wq), (tok_hbm, tok), (g_hbm, gb))
        )
    ]
    for copy in loads:
        copy.start()

    barrier = pltpu.get_barrier_semaphore()
    pl.semaphore_signal(barrier, inc=1, device_id=twin, device_id_type=MESH)
    for n in range(1, 8):
        pl.semaphore_signal(barrier, inc=1, device_id=at_chip(lax.rem(chip + n, 8)), device_id_type=MESH)
    near_same = (dp, (zpos * 2 + 1 - ylo) * 2 + core)
    near_other = (dp + 1 - 2 * lax.rem(dp, 2), (zpos * 2 + 1 - ylo) * 2 + core)

    def greet(device):
        pl.semaphore_signal(barrier, inc=1, device_id=device, device_id_type=MESH)

    @pl.when(core == 0)
    def _():
        for n in range(1, 8):
            for y in range(2):
                greet((lax.rem(dp + n, 8), (zpos * 2 + y) * 2))

    @pl.when(core == 1)
    def _():
        greet(near_other)
        for n in range(1, 4):
            for z in range(4):
                greet((lax.rem(dp + 2 * n, 8), (z * 2 + ylo) * 2 + 1))

    row_at = lax.broadcasted_iota(jnp.int32, (C, C), 0)
    col_at = lax.broadcasted_iota(jnp.int32, (C, C), 1)
    lower = row_at >= col_at
    eye = row_at == col_at

    xpos = lax.div(dp, 2)
    yhi = lax.rem(dp, 2)

    def head_at(n):
        return 2 * lax.rem(xpos + 1 + lax.div(n, 2), 4) + lax.rem(yhi + 1 + n, 2)

    def lanes(h):
        return pl.ds(pl.multiple_of(h * C, C), C)

    upper_ones = jnp.where(row_at <= col_at, 1.0, 0.0).astype(F32)
    for s in range(S):
        sums = lax.dot_general(
            ld_ref[:, s * C : (s + 1) * C], upper_ones, (((1,), (0,)), ((), ())),
            precision=lax.Precision.HIGHEST, preferred_element_type=F32,
        )
        for h in range(H):
            bs[h, s : s + 1, :] = sums[h : h + 1, :]

    loads[0].wait()
    loads[1].wait()

    def local_states(h, carry):
        m_sum = g_sum = None
        decay = None
        for s in range(S):
            rows = slice(s * C, (s + 1) * C)
            across = jnp.broadcast_to(bs[h, s : s + 1, :], (C, C))
            down = across.T
            e = jnp.exp(down)
            el[h, s] = e
            tail = jnp.exp(down[C - 1 : C, :] - down)
            k = kb[rows, lanes(h)]
            kt = (k.astype(F32) * tail).astype(BF16)
            vt = (vb[rows, lanes(h)].astype(F32) * tail).astype(BF16)
            m_new = dot_tn(vt, k)
            g_new = dot_tn(kt, k)
            ll[h, s, 0:C, :] = m_new
            ll[h, s, C : 2 * C, :] = g_new
            last = e[C - 1 : C, :]
            if s == 0:
                m_sum, g_sum, decay = m_new, g_new, last
            else:
                m_sum = last * m_sum + m_new
                g_sum = last * g_sum + g_new
                decay = decay * last
        tile = jnp.broadcast_to(decay, (8, C))
        loc[0, h, 0:C, :] = m_sum
        loc[0, h, C:MSG, :] = tile
        loc[1, h, 0:C, :] = g_sum
        loc[1, h, C:MSG, :] = tile
        return carry

    lax.fori_loop(0, H, local_states, 0)

    pl.semaphore_wait(barrier, jnp.where(core == 0, 22, 21))

    to_twin = remote(loc.at[other], sib, sib_send.at[0], sib_recv.at[0], twin)
    to_twin.start()

    loads[4].wait()

    def tables(h, carry):
        for s in range(S):
            rows = slice(s * C, (s + 1) * C)
            across = jnp.broadcast_to(bs[h, s : s + 1, :], (C, C))
            w = jnp.where(lower, jnp.exp(jnp.where(lower, across.T - across, 0.0)), 0.0)
            wl[h, s] = w
            k = kb[rows, lanes(h)]
            kf = k.astype(F32)
            square = jnp.broadcast_to(jnp.sum(kf * kf, axis=1, keepdims=True), (C, C))
            high = square.astype(BF16)
            low = (square - high.astype(F32)).astype(BF16)
            wb = w.astype(BF16)
            tl[h, s] = dot(jnp.concatenate([wb, wb], axis=1), jnp.concatenate([high, low], axis=0))
            ul[h, s] = (w * dot_nt(gb[rows, lanes(h)], vb[rows, lanes(h)])).astype(BF16)
        return carry

    lax.fori_loop(0, H // 2, tables, 0)

    to_twin.wait_recv()

    def unit(r, u):
        return head_at(4 * r + lax.div(u, 2)), pl.ds(pl.multiple_of(lax.rem(u, 2) * HALF, HALF), HALF)

    def tiles(block):
        return block.reshape(HALF // 8, 8, C)

    def total(r, u):
        h, half = unit(r, u)
        mine_at = loc[core, h, C:MSG, :]
        sib_at = sib[h, C:MSG, :]
        first = core == 0
        by_mine = jnp.where(first, sib_at, 1.0)
        by_sib = jnp.where(first, 1.0, mine_at)
        tot[r, u, HALF : HALF + 8, :] = mine_at * sib_at
        mine, theirs = tiles(loc[core, h, half, :]), tiles(sib[h, half, :])
        tot[r, u, 0:HALF, :] = (by_mine[None] * mine + by_sib[None] * theirs).reshape(HALF, C)

    def forward(r, u):
        return remote(tot.at[r, u], inbox.at[r, chip], fw_send.at[r, u], fw_recv.at[r, chip], at_chip(u))

    def send_totals(r):
        def one(n, carry):
            u = lax.rem(chip + n, 8)
            total(r, u)
            forward(r, u).start()
            return carry

        lax.fori_loop(1, 8, one, 0)
        total(r, chip)
        inbox[r, chip] = tot[r, chip]

    def back(r, c):
        return remote(pre.at[r, c], pin.at[r, chip], bk_send.at[r, c], bk_recv.at[r, chip], at_chip(c))

    def prefix(r):
        state = jnp.zeros((HALF // 8, 8, C), F32)
        for c in range(8):
            pre[r, c] = state.reshape(HALF, C)

            @pl.when(c != chip)
            def _():
                back(r, c).start()
                remote(tot.at[r, c], inbox.at[r, c], fw_send.at[r, c], fw_recv.at[r, c], at_chip(c)).wait_recv()

            state = inbox[r, c, HALF : HALF + 8, :][None] * state + tiles(inbox[r, c, 0:HALF, :])
        pin[r, chip] = pre[r, chip]

    def hand_over(h):
        return remote(snd.at[h], st.at[core, h], st_send.at[h], st_recv.at[h], twin)

    def spread(r):
        def one(e, carry):
            h = head_at(4 * r + e)
            mine_at = loc[core, h, C:MSG, :]
            sib_at = sib[h, C:MSG, :]
            first = core == 0
            for part in range(2):
                u = 2 * e + part
                half = slice(part * HALF, (part + 1) * HALF)

                @pl.when(u != chip)
                def _():
                    remote(pre.at[r, u], pin.at[r, u], bk_send.at[r, u], bk_recv.at[r, u], at_chip(u)).wait_recv()

                base = tiles(pin[r, u])
                mine = mine_at[None] * base + tiles(loc[core, h, half, :])
                theirs = sib_at[None] * base + tiles(sib[h, half, :])
                snd[h, half, :] = jnp.where(first, mine, base).reshape(HALF, C)
                st[core, h, half, :] = jnp.where(first, base, theirs).reshape(HALF, C)
            hand_over(h).start()
            return carry

        lax.fori_loop(0, 4, one, 0)

    send_totals(0)

    lax.fori_loop(H // 2, H, tables, 0)

    prefix(0)

    loads[2].wait()
    loads[3].wait()
    for n in range(H // 2):
        block = dot(tok[...], wq[:, n * 2 * C : (n + 1) * 2 * C]).astype(BF16)
        qb[2 * n] = block[:, 0:C]
        qb[2 * n + 1] = block[:, C : 2 * C]

    send_totals(1)
    spread(0)

    def apply(pq, pg, e, w, state, k):
        p = jnp.concatenate([pq, pg], axis=0).astype(BF16)
        scores = dot_nt(p, k)
        left = jnp.concatenate(
            [
                jnp.concatenate([e * pq, e * pg], axis=0).astype(BF16),
                jnp.concatenate([w * scores[0:C], w * scores[C : 2 * C]], axis=0).astype(BF16),
            ],
            axis=1,
        )
        y = dot(left, jnp.concatenate([state, k], axis=0))
        return y[0:C], y[C : 2 * C]

    def solve(n):
        h = head_at(n)
        ridge = reg_ref[h]
        remote(snd.at[h], st.at[other, h], st_send.at[h], st_recv.at[h], twin).wait_recv()
        m, g = st[0, h], st[1, h]
        trace = jnp.sum(jnp.sum(jnp.where(eye, g, 0.0), axis=0, keepdims=True), axis=1, keepdims=True)
        trace = jnp.broadcast_to(trace, (1, C))
        each = []
        for s in range(S):
            rows = slice(s * C, (s + 1) * C)
            e, w = el[h, s], wl[h, s]
            spans = e * trace + tl[h, s]
            trace = spans[C - 1 : C, :]
            half = 0.5 * spans
            center = ridge + half
            square = half * half
            alpha = 1.0 / center
            alphas, betas = [alpha], [None]
            for step in range(1, ITERS):
                factor = 0.5 if step == 1 else 0.25
                betas.append(factor * (half * alpha) * (half * alpha))
                alpha = 1.0 / (center - factor * square * alpha)
                alphas.append(alpha)
            each.append(dict(rows=rows, e=e, w=w, m=m.astype(BF16), g=g.astype(BF16), a=alphas, b=betas))
            if s + 1 < S:
                last = e[C - 1 : C, :]
                m = last * m + ll[h, s, 0:C, :]
                g = last * g + ll[h, s, C : 2 * C, :]
        for s, t in enumerate(each):
            k = kb[t["rows"], lanes(h)]
            grad = gb[t["rows"], lanes(h)].astype(F32)
            left = jnp.concatenate([(t["e"] * grad).astype(BF16), ul[h, s]], axis=1)
            rg = dot(left, jnp.concatenate([t["m"], k], axis=0))
            rq = qb[h, t["rows"], :].astype(F32)
            t.update(k=k, rq=rq, rg=rg, pq=rq, pg=rg, xq=t["a"][0] * rq, xg=t["a"][0] * rg)
        for step in range(1, ITERS):
            for t in each:
                yq, yg = apply(t["pq"], t["pg"], t["e"], t["w"], t["g"], t["k"])
                before, now, beta = t["a"][step - 1], t["a"][step], t["b"][step]
                for i, y in (("q", yq), ("g", yg)):
                    res = t["r" + i] - before * (ridge * t["p" + i] + y)
                    p = res + beta * t["p" + i]
                    t["r" + i], t["p" + i] = res, p
                    t["x" + i] = t["x" + i] + now * p
        solved = []
        for s, t in enumerate(each):
            scores = dot_nt(t["xq"].astype(BF16), t["k"])
            y = dot_nt((t["e"] * t["xq"]).astype(BF16), t["m"])
            y = y + dot((t["w"] * scores).astype(BF16), vb[t["rows"], lanes(h)])
            mx[t["rows"], lanes(h)] = y.astype(BF16)
            solved.append(t["xg"].T.astype(BF16))
        left = jnp.concatenate(solved, axis=1)
        for c in range(8):
            part = dot(left, tok[:, c * 2 * C : (c + 1) * 2 * C])
            gp[n, 0, c // 2, c % 2] = part[:, 0:C]
            gp[n, 1, c // 2, c % 2] = part[:, C : 2 * C]

    def out_copy(n):
        h = head_at(n)
        return pltpu.make_async_copy(mx.at[:, lanes(h)], mixed_hbm.at[:, lanes(h)], out_sem.at[n])

    def to_core(n):
        return remote(gp.at[n, other], gin.at[n], gs_send.at[n], gs_recv.at[n], twin)

    def far_up(n):
        return remote(gp.at[n, 0, z_far, 0], zc.at[n, 0], zc_send.at[n, 0], zc_recv.at[n, 0], at_z(z_up))

    def far_down(n):
        return remote(gp.at[n, 0, z_far, 1], zc.at[n, 1], zc_send.at[n, 1], zc_recv.at[n, 1], at_z(z_down))

    def near_up(n):
        return remote(gp.at[n, 0, z_up], za.at[n, 0], za_send.at[n, 0], za_recv.at[n, 0], at_z(z_up))

    def near_down(n):
        return remote(gp.at[n, 0, z_down], za.at[n, 1], za_send.at[n, 1], za_recv.at[n, 1], at_z(z_down))

    def finish_z(n, y):
        at = dp * 2 + ylo
        return remote(
            gp.at[n, 0, zpos, y], fin.at[at], fin_send.at[n, y], fin_recv.at[at], (head_at(n), (zpos * 2 + y) * 2)
        )

    def far_same(n):
        return remote(
            gp.at[n, 1, 0:2, ylo], zc.at[n], zc_send.at[n, 0], zc_recv.at[n, 0], near_same
        )

    def far_other(n):
        return remote(
            gp.at[n, 1, 2:4, ylo], zc.at[n + 1], zc_send.at[n, 1], zc_recv.at[n, 1], near_other
        )

    def send_other(n):
        return remote(gp.at[n, 1, :, 1 - ylo], ya.at[n], za_send.at[n, 0], za_recv.at[n, 0], near_other)

    def send_same(n):
        return remote(gp.at[n, 1, :, 1 - ylo], ya.at[n], za_send.at[n, 0], za_recv.at[n, 0], near_same)

    def finish_y(n, z):
        at = xpos * 4 + zpos
        return remote(
            gp.at[n, 1, z, ylo], fin.at[at], fin_send.at[n, z], fin_recv.at[at], (head_at(n), (z * 2 + ylo) * 2 + 1)
        )

    def odd(n):
        return lax.rem(n, 2) == 1

    def even(n):
        return lax.rem(n, 2) == 0

    def turn(i, carry):
        @pl.when(i == 1)
        def _():
            prefix(1)

        @pl.when(i == 3)
        def _():
            spread(1)

        @pl.when(i < H)
        def _():
            solve(i)
            to_core(i).start()
            out_copy(i).start()

        n1, n2, n3, n4 = i - 1, i - FAR, i - NEAR, i - SAME
        in1 = (i >= 1) & (i < H + 1)
        in2 = (i >= FAR) & (i < H + FAR)
        in3 = (i >= NEAR) & (i < H + NEAR)
        in4 = (i >= SAME) & (i < H + SAME)

        @pl.when(in1)
        def _():
            to_core(n1).wait_recv()
            gp[n1, core] = gp[n1, core] + gin[n1]

        @pl.when(in1 & (core == 0))
        def _():
            far_up(n1).start()
            far_down(n1).start()

        @pl.when(in2 & (core == 0))
        def _():
            far_up(n2).wait_recv()
            far_down(n2).wait_recv()
            gp[n2, 0, z_up, 0] = gp[n2, 0, z_up, 0] + zc[n2, 0]
            gp[n2, 0, z_down, 1] = gp[n2, 0, z_down, 1] + zc[n2, 1]
            near_up(n2).start()
            near_down(n2).start()

        @pl.when(in3 & (core == 0))
        def _():
            near_up(n3).wait_recv()
            near_down(n3).wait_recv()
            for y in range(2):
                gp[n3, 0, zpos, y] = gp[n3, 0, zpos, y] + za[n3, 0, y] + za[n3, 1, y]

                @pl.when((n3 < H - 1) | (ylo != y))
                def _():
                    finish_z(n3, y).start()

                @pl.when((n3 == H - 1) & (ylo == y))
                def _():
                    fin[dp * 2 + y] = gp[n3, 0, zpos, y]

        @pl.when(in1 & (core == 1) & even(n1))
        def _():
            far_same(n1).start()
            far_other(n1).start()

        @pl.when(in4 & (core == 1) & odd(n4))
        def _():
            far_other(n4 - 1).wait_recv()
            gp[n4, 1, 2:4, 1 - ylo] = gp[n4, 1, 2:4, 1 - ylo] + zc[n4]
            send_same(n4).start()

        @pl.when(in2 & (core == 1) & even(n2))
        def _():
            far_same(n2).wait_recv()
            gp[n2, 1, 0:2, 1 - ylo] = gp[n2, 1, 0:2, 1 - ylo] + zc[n2]
            send_other(n2).start()

        @pl.when(in3 & (core == 1) & odd(n3))
        def _():
            send_other(n3 - 1).wait_recv()
            send_same(n3).wait_recv()
            for z in range(4):
                gp[n3, 1, z, ylo] = gp[n3, 1, z, ylo] + ya[n3 - 1, z] + ya[n3, z]

                @pl.when((n3 < H - 1) | (zpos != z))
                def _():
                    finish_y(n3, z).start()

                @pl.when((n3 == H - 1) & (zpos == z))
                def _():
                    fin[xpos * 4 + z] = gp[n3, 1, z, ylo]

        return carry

    lax.fori_loop(0, H + NEAR, turn, 0)

    acc = None
    own = jnp.where(core == 0, dp * 2 + ylo, xpos * 4 + zpos)
    for source in range(16):

        @pl.when(own != source)
        def _():
            remote(gp.at[0, 0, 0, 0], fin.at[source], fin_send.at[0, 0], fin_recv.at[source], twin).wait_recv()

        acc = fin[source] if acc is None else acc + fin[source]
    qg_ref[...] = acc

    to_twin.wait_send()

    def drain(n, carry):
        @pl.when(n != chip)
        def _():
            for r in range(2):
                forward(r, n).wait_send()
                back(r, n).wait_send()

        hand_over(n).wait_send()
        out_copy(n).wait()
        to_core(n).wait_send()

        @pl.when(core == 0)
        def _():
            far_up(n).wait_send()
            far_down(n).wait_send()
            near_up(n).wait_send()
            near_down(n).wait_send()
            for y in range(2):

                @pl.when((n < H - 1) | (ylo != y))
                def _():
                    finish_z(n, y).wait_send()

        @pl.when((core == 1) & even(n))
        def _():
            far_same(n).wait_send()
            far_other(n).wait_send()
            send_other(n).wait_send()

        @pl.when((core == 1) & odd(n))
        def _():
            send_same(n).wait_send()
            for z in range(4):

                @pl.when((n < H - 1) | (zpos != z))
                def _():
                    finish_y(n, z).wait_send()

        return carry

    lax.fori_loop(0, H, drain, 0)


def per_device(tokens, w_query, keys, values, log_decay, regular, grad_out):
    dma = pltpu.SemaphoreType.DMA
    hbm = pl.BlockSpec(memory_space=pl.ANY)
    vmem = pl.BlockSpec(memory_space=pltpu.VMEM)
    smem = pl.BlockSpec(memory_space=pltpu.SMEM)
    mixed, query_grad = pl.pallas_call(
        kernel,
        out_shape=(
            jax.ShapeDtypeStruct((ROWS, H * C), BF16),
            jax.ShapeDtypeStruct((C, C), F32),
        ),
        in_specs=[hbm, hbm, hbm, hbm, vmem, smem, hbm],
        out_specs=(hbm, vmem),
        scratch_shapes=[
            pltpu.VMEM((ROWS, D), BF16),
            pltpu.VMEM((D, H * C), BF16),
            pltpu.VMEM((ROWS, H * C), BF16),
            pltpu.VMEM((ROWS, H * C), BF16),
            pltpu.VMEM((ROWS, H * C), BF16),
            pltpu.VMEM((H, ROWS, C), BF16),
            pltpu.VMEM((ROWS, H * C), BF16),
            pltpu.VMEM((H, S, C), F32),
            pltpu.VMEM((H, S, C, C), F32),
            pltpu.VMEM((H, S, C, C), F32),
            pltpu.VMEM((H, S, C, C), F32),
            pltpu.VMEM((H, S, C, C), BF16),
            pltpu.VMEM((H, S, 2 * C, C), F32),
            pltpu.VMEM((2, H, MSG, C), F32),
            pltpu.VMEM((H, MSG, C), F32),
            pltpu.VMEM((2, 8, HALF + 8, C), F32),
            pltpu.VMEM((2, 8, HALF + 8, C), F32),
            pltpu.VMEM((2, 8, HALF, C), F32),
            pltpu.VMEM((2, 8, HALF, C), F32),
            pltpu.VMEM((H, C, C), F32),
            pltpu.VMEM((2, H, C, C), F32),
            pltpu.VMEM((H, 2, 4, 2, C, C), F32),
            pltpu.VMEM((H, 4, 2, C, C), F32),
            pltpu.VMEM((H, 2, C, C), F32),
            pltpu.VMEM((H, 2, 2, C, C), F32),
            pltpu.VMEM((H, 4, C, C), F32),
            pltpu.VMEM((16, C, C), F32),
            dma((5,)),
            dma((H,)),
            dma((1,)),
            dma((1,)),
            dma((2, 8)),
            dma((2, 8)),
            dma((2, 8)),
            dma((2, 8)),
            dma((H,)),
            dma((H,)),
            dma((H,)),
            dma((H,)),
            dma((H, 2)),
            dma((H, 2)),
            dma((H, 2)),
            dma((H, 2)),
            dma((H, 4)),
            dma((16,)),
        ],
        compiler_params=pltpu.CompilerParams(
            collective_id=0, has_side_effects=True, vmem_limit_bytes=60 * 2**20
        ),
    )(
        tokens.reshape(ROWS, D),
        w_query,
        keys.reshape(ROWS, H * C),
        values.reshape(ROWS, H * C),
        log_decay.reshape(H, ROWS),
        regular,
        grad_out.reshape(ROWS, H * C),
    )
    parts = 4
    step = ROWS // parts

    def move(a_ref, b_ref, c_ref, d_ref, held, sums, sem_in, sem_out):
        def a_copy(n):
            rows = pl.ds(n * step, step)
            return (
                pltpu.make_async_copy(a_ref.at[rows], held.at[rows], sem_in.at[n]),
                pltpu.make_async_copy(held.at[rows], c_ref.at[rows], sem_out.at[n]),
            )

        pairs = [a_copy(n) for n in range(parts)]
        pairs.append(
            (
                pltpu.make_async_copy(b_ref, sums, sem_in.at[parts]),
                pltpu.make_async_copy(sums, d_ref, sem_out.at[parts]),
            )
        )
        for come, _ in pairs:
            come.start()
        for come, go in pairs:
            come.wait()
            go.start()
        for _, go in pairs:
            go.wait()

    mixed, query_grad = pl.pallas_call(
        move,
        out_shape=(jax.ShapeDtypeStruct(mixed.shape, BF16), jax.ShapeDtypeStruct(query_grad.shape, F32)),
        in_specs=[hbm, hbm],
        out_specs=(hbm, hbm),
        scratch_shapes=[
            pltpu.VMEM((ROWS, H * C), BF16),
            pltpu.VMEM((C, C), F32),
            dma((parts + 1,)),
            dma((parts + 1,)),
        ],
    )(mixed, query_grad)
    return mixed.reshape(1, ROWS, H * C), query_grad


def solution(mesh):
    in_specs = (
        P("dp", "seq", None),
        P(),
        P("dp", "seq", None),
        P("dp", "seq", None),
        P("dp", None, "seq"),
        P(),
        P("dp", "seq", None),
    )
    out_specs = (P("dp", "seq", None), P("dp", "seq"))
    return jax.shard_map(
        per_device, mesh=mesh, in_specs=in_specs, out_specs=out_specs, check_vma=False
    )
```

```python
import functools

import jax
import jax.numpy as jnp
from jax import lax
from jax.experimental import pallas as pl
from jax.experimental.pallas import tpu as pltpu
from jax.sharding import PartitionSpec as P

F32 = jnp.float32
BF16 = jnp.bfloat16
MESH = pl.DeviceIdType.MESH

H = 8
C = 128
S = 4
ROWS = S * C
D = 2048
MSG = C + 8
HALF = C // 2
ITERS = 4
FAR, SAME, NEAR = 3, 2, 5


def dot(a, b):
    return lax.dot_general(a, b, (((1,), (0,)), ((), ())), preferred_element_type=F32)


def dot_nt(a, b):
    return lax.dot_general(a, b, (((1,), (1,)), ((), ())), preferred_element_type=F32)


def dot_tn(a, b):
    return lax.dot_general(a, b, (((0,), (0,)), ((), ())), preferred_element_type=F32)


def kernel(
    tok_hbm, wq_hbm, k_hbm, v_hbm, ld_ref, reg_ref, g_hbm,
    mixed_hbm, qg_ref,
    tok, wq, kb, vb, gb, qb, mx,
    bs, el, wl, tl, ul, ll,
    loc, sib, tot, inbox, pre, pin, snd, st,
    gp, gin, zc, za, ya, fin,
    load_sem, out_sem,
    sib_send, sib_recv, fw_send, fw_recv, bk_send, bk_recv, st_send, st_recv,
    gs_send, gs_recv, zc_send, zc_recv, za_send, za_recv, fin_send, fin_recv,
):
    dp = lax.axis_index("dp")
    seq = lax.axis_index("seq")
    core = lax.rem(seq, 2)
    other = 1 - core
    chip = lax.div(seq, 2)
    zpos = lax.div(chip, 2)
    ylo = lax.rem(chip, 2)
    twin = (dp, chip * 2 + other)

    def at_chip(c):
        return (dp, c * 2 + core)

    def at_z(z):
        return (dp, (z * 2 + ylo) * 2 + core)

    z_up = lax.rem(zpos + 1, 4)
    z_down = lax.rem(zpos + 3, 4)
    z_far = lax.rem(zpos + 2, 4)

    def remote(src, dst, send, recv, device):
        return pltpu.make_async_remote_copy(
            src_ref=src, dst_ref=dst, send_sem=send, recv_sem=recv, device_id=device, device_id_type=MESH
        )

    loads = [
        pltpu.make_async_copy(src, dst, load_sem.at[n])
        for n, (src, dst) in enumerate(
            ((k_hbm, kb), (v_hbm, vb), (wq_hbm, wq), (tok_hbm, tok), (g_hbm, gb))
        )
    ]
    loads[0].start()
    loads[1].start()

    barrier = pltpu.get_barrier_semaphore()
    pl.semaphore_signal(barrier, inc=1, device_id=twin, device_id_type=MESH)
    for n in range(1, 8):
        pl.semaphore_signal(barrier, inc=1, device_id=at_chip(lax.rem(chip + n, 8)), device_id_type=MESH)
    near_same = (dp, (zpos * 2 + 1 - ylo) * 2 + core)
    near_other = (dp + 1 - 2 * lax.rem(dp, 2), (zpos * 2 + 1 - ylo) * 2 + core)

    def greet(device):
        pl.semaphore_signal(barrier, inc=1, device_id=device, device_id_type=MESH)

    @pl.when(core == 0)
    def _():
        for n in range(1, 8):
            for y in range(2):
                greet((lax.rem(dp + n, 8), (zpos * 2 + y) * 2))

    @pl.when(core == 1)
    def _():
        greet(near_other)
        for n in range(1, 4):
            for z in range(4):
                greet((lax.rem(dp + 2 * n, 8), (z * 2 + ylo) * 2 + 1))

    row_at = lax.broadcasted_iota(jnp.int32, (C, C), 0)
    col_at = lax.broadcasted_iota(jnp.int32, (C, C), 1)
    lower = row_at >= col_at
    eye = row_at == col_at

    xpos = lax.div(dp, 2)
    yhi = lax.rem(dp, 2)

    def head_at(n):
        return 2 * lax.rem(xpos + 1 + lax.div(n, 2), 4) + lax.rem(yhi + 1 + n, 2)

    def lanes(h):
        return pl.ds(pl.multiple_of(h * C, C), C)

    upper_ones = jnp.where(row_at <= col_at, 1.0, 0.0).astype(F32)
    for s in range(S):
        sums = lax.dot_general(
            ld_ref[:, s * C : (s + 1) * C], upper_ones, (((1,), (0,)), ((), ())),
            precision=lax.Precision.HIGHEST, preferred_element_type=F32,
        )
        for h in range(H):
            bs[h, s : s + 1, :] = sums[h : h + 1, :]

    loads[0].wait()
    loads[1].wait()
    for copy in (loads[4], loads[3], loads[2]):
        copy.start()

    def local_states(n, carry):
        h = head_at(n)
        m_sum = g_sum = None
        decay = None
        for s in range(S):
            rows = slice(s * C, (s + 1) * C)
            across = jnp.broadcast_to(bs[h, s : s + 1, :], (C, C))
            down = across.T
            e = jnp.exp(down)
            el[h, s] = e
            tail = jnp.exp(down[C - 1 : C, :] - down)
            k = kb[rows, lanes(h)]
            kt = (k.astype(F32) * tail).astype(BF16)
            vt = (vb[rows, lanes(h)].astype(F32) * tail).astype(BF16)
            m_new = dot_tn(vt, k)
            g_new = dot_tn(kt, k)
            ll[h, s, 0:C, :] = m_new
            ll[h, s, C : 2 * C, :] = g_new
            last = e[C - 1 : C, :]
            if s == 0:
                m_sum, g_sum, decay = m_new, g_new, last
            else:
                m_sum = last * m_sum + m_new
                g_sum = last * g_sum + g_new
                decay = decay * last
        tile = jnp.broadcast_to(decay, (8, C))
        loc[0, n, 0:C, :] = m_sum
        loc[0, n, C:MSG, :] = tile
        loc[1, n, 0:C, :] = g_sum
        loc[1, n, C:MSG, :] = tile
        return carry

    lax.fori_loop(0, 4, local_states, 0)

    pl.semaphore_wait(barrier, jnp.where(core == 0, 22, 21))

    def to_twin(r):
        four = pl.ds(4 * r, 4)
        return remote(loc.at[other, four], sib.at[four], sib_send.at[r], sib_recv.at[r], twin)

    to_twin(0).start()

    lax.fori_loop(4, H, local_states, 0)
    to_twin(1).start()

    loads[4].wait()

    def tables(h, carry):
        for s in range(S):
            rows = slice(s * C, (s + 1) * C)
            across = jnp.broadcast_to(bs[h, s : s + 1, :], (C, C))
            w = jnp.where(lower, jnp.exp(jnp.where(lower, across.T - across, 0.0)), 0.0)
            wl[h, s] = w
            k = kb[rows, lanes(h)]
            kf = k.astype(F32)
            square = jnp.broadcast_to(jnp.sum(kf * kf, axis=1, keepdims=True), (C, C))
            high = square.astype(BF16)
            low = (square - high.astype(F32)).astype(BF16)
            wb = w.astype(BF16)
            tl[h, s] = dot(jnp.concatenate([wb, wb], axis=1), jnp.concatenate([high, low], axis=0))
            ul[h, s] = (w * dot_nt(gb[rows, lanes(h)], vb[rows, lanes(h)])).astype(BF16)
        return carry

    def unit(r, u):
        return 4 * r + lax.div(u, 2), pl.ds(pl.multiple_of(lax.rem(u, 2) * HALF, HALF), HALF)

    def tiles(block):
        return block.reshape(HALF // 8, 8, C)

    def total(r, u):
        n, half = unit(r, u)
        mine_at = loc[core, n, C:MSG, :]
        sib_at = sib[n, C:MSG, :]
        first = core == 0
        by_mine = jnp.where(first, sib_at, 1.0)
        by_sib = jnp.where(first, 1.0, mine_at)
        tot[r, u, HALF : HALF + 8, :] = mine_at * sib_at
        mine, theirs = tiles(loc[core, n, half, :]), tiles(sib[n, half, :])
        tot[r, u, 0:HALF, :] = (by_mine[None] * mine + by_sib[None] * theirs).reshape(HALF, C)

    def forward(r, u):
        return remote(tot.at[r, u], inbox.at[r, chip], fw_send.at[r, u], fw_recv.at[r, chip], at_chip(u))

    def send_totals(r):
        def one(n, carry):
            u = lax.rem(chip + n, 8)
            total(r, u)
            forward(r, u).start()
            return carry

        lax.fori_loop(1, 8, one, 0)
        total(r, chip)
        inbox[r, chip] = tot[r, chip]

    def back(r, c):
        return remote(pre.at[r, c], pin.at[r, chip], bk_send.at[r, c], bk_recv.at[r, chip], at_chip(c))

    def prefix(r):
        state = jnp.zeros((HALF // 8, 8, C), F32)
        for c in range(8):
            pre[r, c] = state.reshape(HALF, C)

            @pl.when(c != chip)
            def _():
                back(r, c).start()
                remote(tot.at[r, c], inbox.at[r, c], fw_send.at[r, c], fw_recv.at[r, c], at_chip(c)).wait_recv()

            state = inbox[r, c, HALF : HALF + 8, :][None] * state + tiles(inbox[r, c, 0:HALF, :])
        pin[r, chip] = pre[r, chip]

    def hand_over(h):
        return remote(snd.at[h], st.at[core, h], st_send.at[h], st_recv.at[h], twin)

    def spread(r):
        def one(e, carry):
            n = 4 * r + e
            h = head_at(n)
            mine_at = loc[core, n, C:MSG, :]
            sib_at = sib[n, C:MSG, :]
            first = core == 0
            for part in range(2):
                u = 2 * e + part
                half = slice(part * HALF, (part + 1) * HALF)

                @pl.when(u != chip)
                def _():
                    remote(pre.at[r, u], pin.at[r, u], bk_send.at[r, u], bk_recv.at[r, u], at_chip(u)).wait_recv()

                base = tiles(pin[r, u])
                mine = mine_at[None] * base + tiles(loc[core, n, half, :])
                theirs = sib_at[None] * base + tiles(sib[n, half, :])
                snd[h, half, :] = jnp.where(first, mine, base).reshape(HALF, C)
                st[core, h, half, :] = jnp.where(first, base, theirs).reshape(HALF, C)
            hand_over(h).start()
            return carry

        lax.fori_loop(0, 4, one, 0)

    to_twin(0).wait_recv()
    send_totals(0)

    lax.fori_loop(0, H, tables, 0)

    prefix(0)

    loads[2].wait()
    loads[3].wait()
    for n in range(H // 2):
        block = dot(tok[...], wq[:, n * 2 * C : (n + 1) * 2 * C]).astype(BF16)
        qb[2 * n] = block[:, 0:C]
        qb[2 * n + 1] = block[:, C : 2 * C]

    to_twin(1).wait_recv()
    send_totals(1)
    spread(0)

    def apply(pq, pg, e, w, state, k):
        p = jnp.concatenate([pq, pg], axis=0).astype(BF16)
        scores = dot_nt(p, k)
        left = jnp.concatenate(
            [
                jnp.concatenate([e * pq, e * pg], axis=0).astype(BF16),
                jnp.concatenate([w * scores[0:C], w * scores[C : 2 * C]], axis=0).astype(BF16),
            ],
            axis=1,
        )
        y = dot(left, jnp.concatenate([state, k], axis=0))
        return y[0:C], y[C : 2 * C]

    def solve(n):
        h = head_at(n)
        ridge = reg_ref[h]
        remote(snd.at[h], st.at[other, h], st_send.at[h], st_recv.at[h], twin).wait_recv()
        m, g = st[0, h], st[1, h]
        trace = jnp.sum(jnp.sum(jnp.where(eye, g, 0.0), axis=0, keepdims=True), axis=1, keepdims=True)
        trace = jnp.broadcast_to(trace, (1, C))
        each = []
        for s in range(S):
            rows = slice(s * C, (s + 1) * C)
            e, w = el[h, s], wl[h, s]
            spans = e * trace + tl[h, s]
            trace = spans[C - 1 : C, :]
            half = 0.5 * spans
            center = ridge + half
            square = half * half
            alpha = 1.0 / center
            alphas, betas = [alpha], [None]
            for step in range(1, ITERS):
                factor = 0.5 if step == 1 else 0.25
                betas.append(factor * (half * alpha) * (half * alpha))
                alpha = 1.0 / (center - factor * square * alpha)
                alphas.append(alpha)
            each.append(dict(rows=rows, e=e, w=w, m=m.astype(BF16), g=g.astype(BF16), a=alphas, b=betas))
            if s + 1 < S:
                last = e[C - 1 : C, :]
                m = last * m + ll[h, s, 0:C, :]
                g = last * g + ll[h, s, C : 2 * C, :]
        for s, t in enumerate(each):
            k = kb[t["rows"], lanes(h)]
            grad = gb[t["rows"], lanes(h)].astype(F32)
            left = jnp.concatenate([(t["e"] * grad).astype(BF16), ul[h, s]], axis=1)
            rg = dot(left, jnp.concatenate([t["m"], k], axis=0))
            rq = qb[h, t["rows"], :].astype(F32)
            t.update(k=k, rq=rq, rg=rg, pq=rq, pg=rg, xq=t["a"][0] * rq, xg=t["a"][0] * rg)
        for step in range(1, ITERS):
            for t in each:
                yq, yg = apply(t["pq"], t["pg"], t["e"], t["w"], t["g"], t["k"])
                before, now, beta = t["a"][step - 1], t["a"][step], t["b"][step]
                for i, y in (("q", yq), ("g", yg)):
                    res = t["r" + i] - before * (ridge * t["p" + i] + y)
                    p = res + beta * t["p" + i]
                    t["r" + i], t["p" + i] = res, p
                    t["x" + i] = t["x" + i] + now * p
        solved = []
        for s, t in enumerate(each):
            scores = dot_nt(t["xq"].astype(BF16), t["k"])
            y = dot_nt((t["e"] * t["xq"]).astype(BF16), t["m"])
            y = y + dot((t["w"] * scores).astype(BF16), vb[t["rows"], lanes(h)])
            mx[t["rows"], lanes(h)] = y.astype(BF16)
            solved.append(t["xg"].T.astype(BF16))
        left = jnp.concatenate(solved, axis=1)
        for c in range(8):
            part = dot(left, tok[:, c * 2 * C : (c + 1) * 2 * C])
            gp[n, 0, c // 2, c % 2] = part[:, 0:C]
            gp[n, 1, c // 2, c % 2] = part[:, C : 2 * C]

    def out_copy(n):
        h = head_at(n)
        return pltpu.make_async_copy(mx.at[:, lanes(h)], mixed_hbm.at[:, lanes(h)], out_sem.at[n])

    def to_core(n):
        return remote(gp.at[n, other], gin.at[n], gs_send.at[n], gs_recv.at[n], twin)

    def far_up(n):
        return remote(gp.at[n, 0, z_far, 0], zc.at[n, 0], zc_send.at[n, 0], zc_recv.at[n, 0], at_z(z_up))

    def far_down(n):
        return remote(gp.at[n, 0, z_far, 1], zc.at[n, 1], zc_send.at[n, 1], zc_recv.at[n, 1], at_z(z_down))

    def near_up(n):
        return remote(gp.at[n, 0, z_up], za.at[n, 0], za_send.at[n, 0], za_recv.at[n, 0], at_z(z_up))

    def near_down(n):
        return remote(gp.at[n, 0, z_down], za.at[n, 1], za_send.at[n, 1], za_recv.at[n, 1], at_z(z_down))

    def finish_z(n, y):
        at = dp * 2 + ylo
        return remote(
            gp.at[n, 0, zpos, y], fin.at[at], fin_send.at[n, y], fin_recv.at[at], (head_at(n), (zpos * 2 + y) * 2)
        )

    def far_same(n):
        return remote(
            gp.at[n, 1, 0:2, ylo], zc.at[n], zc_send.at[n, 0], zc_recv.at[n, 0], near_same
        )

    def far_other(n):
        return remote(
            gp.at[n, 1, 2:4, ylo], zc.at[n + 1], zc_send.at[n, 1], zc_recv.at[n, 1], near_other
        )

    def send_other(n):
        return remote(gp.at[n, 1, :, 1 - ylo], ya.at[n], za_send.at[n, 0], za_recv.at[n, 0], near_other)

    def send_same(n):
        return remote(gp.at[n, 1, :, 1 - ylo], ya.at[n], za_send.at[n, 0], za_recv.at[n, 0], near_same)

    def finish_y(n, z):
        at = xpos * 4 + zpos
        return remote(
            gp.at[n, 1, z, ylo], fin.at[at], fin_send.at[n, z], fin_recv.at[at], (head_at(n), (z * 2 + ylo) * 2 + 1)
        )

    def odd(n):
        return lax.rem(n, 2) == 1

    def even(n):
        return lax.rem(n, 2) == 0

    def turn(i, carry):
        @pl.when(i == 1)
        def _():
            prefix(1)

        @pl.when(i == 3)
        def _():
            spread(1)

        @pl.when(i < H)
        def _():
            solve(i)
            to_core(i).start()
            out_copy(i).start()

        n1, n2, n3, n4 = i - 1, i - FAR, i - NEAR, i - SAME
        in1 = (i >= 1) & (i < H + 1)
        in2 = (i >= FAR) & (i < H + FAR)
        in3 = (i >= NEAR) & (i < H + NEAR)
        in4 = (i >= SAME) & (i < H + SAME)

        @pl.when(in1)
        def _():
            to_core(n1).wait_recv()
            gp[n1, core] = gp[n1, core] + gin[n1]

        @pl.when(in1 & (core == 0))
        def _():
            far_up(n1).start()
            far_down(n1).start()

        @pl.when(in2 & (core == 0))
        def _():
            far_up(n2).wait_recv()
            far_down(n2).wait_recv()
            gp[n2, 0, z_up, 0] = gp[n2, 0, z_up, 0] + zc[n2, 0]
            gp[n2, 0, z_down, 1] = gp[n2, 0, z_down, 1] + zc[n2, 1]
            near_up(n2).start()
            near_down(n2).start()

        @pl.when(in3 & (core == 0))
        def _():
            near_up(n3).wait_recv()
            near_down(n3).wait_recv()
            for y in range(2):
                gp[n3, 0, zpos, y] = gp[n3, 0, zpos, y] + za[n3, 0, y] + za[n3, 1, y]

                @pl.when((n3 < H - 1) | (ylo != y))
                def _():
                    finish_z(n3, y).start()

                @pl.when((n3 == H - 1) & (ylo == y))
                def _():
                    fin[dp * 2 + y] = gp[n3, 0, zpos, y]

        @pl.when(in1 & (core == 1) & even(n1))
        def _():
            far_same(n1).start()
            far_other(n1).start()

        @pl.when(in4 & (core == 1) & odd(n4))
        def _():
            far_other(n4 - 1).wait_recv()
            gp[n4, 1, 2:4, 1 - ylo] = gp[n4, 1, 2:4, 1 - ylo] + zc[n4]
            send_same(n4).start()

        @pl.when(in2 & (core == 1) & even(n2))
        def _():
            far_same(n2).wait_recv()
            gp[n2, 1, 0:2, 1 - ylo] = gp[n2, 1, 0:2, 1 - ylo] + zc[n2]
            send_other(n2).start()

        @pl.when(in3 & (core == 1) & odd(n3))
        def _():
            send_other(n3 - 1).wait_recv()
            send_same(n3).wait_recv()
            for z in range(4):
                gp[n3, 1, z, ylo] = gp[n3, 1, z, ylo] + ya[n3 - 1, z] + ya[n3, z]

                @pl.when((n3 < H - 1) | (zpos != z))
                def _():
                    finish_y(n3, z).start()

                @pl.when((n3 == H - 1) & (zpos == z))
                def _():
                    fin[xpos * 4 + z] = gp[n3, 1, z, ylo]

        return carry

    lax.fori_loop(0, H + NEAR, turn, 0)

    acc = None
    own = jnp.where(core == 0, dp * 2 + ylo, xpos * 4 + zpos)
    for source in range(16):

        @pl.when(own != source)
        def _():
            remote(gp.at[0, 0, 0, 0], fin.at[source], fin_send.at[0, 0], fin_recv.at[source], twin).wait_recv()

        acc = fin[source] if acc is None else acc + fin[source]
    qg_ref[...] = acc

    to_twin(0).wait_send()
    to_twin(1).wait_send()

    def drain(n, carry):
        @pl.when(n != chip)
        def _():
            for r in range(2):
                forward(r, n).wait_send()
                back(r, n).wait_send()

        hand_over(n).wait_send()
        out_copy(n).wait()
        to_core(n).wait_send()

        @pl.when(core == 0)
        def _():
            far_up(n).wait_send()
            far_down(n).wait_send()
            near_up(n).wait_send()
            near_down(n).wait_send()
            for y in range(2):

                @pl.when((n < H - 1) | (ylo != y))
                def _():
                    finish_z(n, y).wait_send()

        @pl.when((core == 1) & even(n))
        def _():
            far_same(n).wait_send()
            far_other(n).wait_send()
            send_other(n).wait_send()

        @pl.when((core == 1) & odd(n))
        def _():
            send_same(n).wait_send()
            for z in range(4):

                @pl.when((n < H - 1) | (zpos != z))
                def _():
                    finish_y(n, z).wait_send()

        return carry

    lax.fori_loop(0, H, drain, 0)


def per_device(tokens, w_query, keys, values, log_decay, regular, grad_out):
    dma = pltpu.SemaphoreType.DMA
    hbm = pl.BlockSpec(memory_space=pl.ANY)
    vmem = pl.BlockSpec(memory_space=pltpu.VMEM)
    smem = pl.BlockSpec(memory_space=pltpu.SMEM)
    mixed, query_grad = pl.pallas_call(
        kernel,
        out_shape=(
            jax.ShapeDtypeStruct((ROWS, H * C), BF16),
            jax.ShapeDtypeStruct((C, C), F32),
        ),
        in_specs=[hbm, hbm, hbm, hbm, vmem, smem, hbm],
        out_specs=(hbm, vmem),
        scratch_shapes=[
            pltpu.VMEM((ROWS, D), BF16),
            pltpu.VMEM((D, H * C), BF16),
            pltpu.VMEM((ROWS, H * C), BF16),
            pltpu.VMEM((ROWS, H * C), BF16),
            pltpu.VMEM((ROWS, H * C), BF16),
            pltpu.VMEM((H, ROWS, C), BF16),
            pltpu.VMEM((ROWS, H * C), BF16),
            pltpu.VMEM((H, S, C), F32),
            pltpu.VMEM((H, S, C, C), F32),
            pltpu.VMEM((H, S, C, C), F32),
            pltpu.VMEM((H, S, C, C), F32),
            pltpu.VMEM((H, S, C, C), BF16),
            pltpu.VMEM((H, S, 2 * C, C), F32),
            pltpu.VMEM((2, H, MSG, C), F32),
            pltpu.VMEM((H, MSG, C), F32),
            pltpu.VMEM((2, 8, HALF + 8, C), F32),
            pltpu.VMEM((2, 8, HALF + 8, C), F32),
            pltpu.VMEM((2, 8, HALF, C), F32),
            pltpu.VMEM((2, 8, HALF, C), F32),
            pltpu.VMEM((H, C, C), F32),
            pltpu.VMEM((2, H, C, C), F32),
            pltpu.VMEM((H, 2, 4, 2, C, C), F32),
            pltpu.VMEM((H, 4, 2, C, C), F32),
            pltpu.VMEM((H, 2, C, C), F32),
            pltpu.VMEM((H, 2, 2, C, C), F32),
            pltpu.VMEM((H, 4, C, C), F32),
            pltpu.VMEM((16, C, C), F32),
            dma((5,)),
            dma((H,)),
            dma((2,)),
            dma((2,)),
            dma((2, 8)),
            dma((2, 8)),
            dma((2, 8)),
            dma((2, 8)),
            dma((H,)),
            dma((H,)),
            dma((H,)),
            dma((H,)),
            dma((H, 2)),
            dma((H, 2)),
            dma((H, 2)),
            dma((H, 2)),
            dma((H, 4)),
            dma((16,)),
        ],
        compiler_params=pltpu.CompilerParams(
            collective_id=0, has_side_effects=True, vmem_limit_bytes=60 * 2**20
        ),
    )(
        tokens.reshape(ROWS, D),
        w_query,
        keys.reshape(ROWS, H * C),
        values.reshape(ROWS, H * C),
        log_decay.reshape(H, ROWS),
        regular,
        grad_out.reshape(ROWS, H * C),
    )
    parts = 4
    step = ROWS // parts

    def move(a_ref, b_ref, c_ref, d_ref, held, sums, sem_in, sem_out):
        def a_copy(n):
            rows = pl.ds(n * step, step)
            return (
                pltpu.make_async_copy(a_ref.at[rows], held.at[rows], sem_in.at[n]),
                pltpu.make_async_copy(held.at[rows], c_ref.at[rows], sem_out.at[n]),
            )

        pairs = [a_copy(n) for n in range(parts)]
        pairs.append(
            (
                pltpu.make_async_copy(b_ref, sums, sem_in.at[parts]),
                pltpu.make_async_copy(sums, d_ref, sem_out.at[parts]),
            )
        )
        for come, _ in pairs:
            come.start()
        for come, go in pairs:
            come.wait()
            go.start()
        for _, go in pairs:
            go.wait()

    mixed, query_grad = pl.pallas_call(
        move,
        out_shape=(jax.ShapeDtypeStruct(mixed.shape, BF16), jax.ShapeDtypeStruct(query_grad.shape, F32)),
        in_specs=[hbm, hbm],
        out_specs=(hbm, hbm),
        scratch_shapes=[
            pltpu.VMEM((ROWS, H * C), BF16),
            pltpu.VMEM((C, C), F32),
            dma((parts + 1,)),
            dma((parts + 1,)),
        ],
    )(mixed, query_grad)
    return mixed.reshape(1, ROWS, H * C), query_grad


def solution(mesh):
    in_specs = (
        P("dp", "seq", None),
        P(),
        P("dp", "seq", None),
        P("dp", "seq", None),
        P("dp", None, "seq"),
        P(),
        P("dp", "seq", None),
    )
    out_specs = (P("dp", "seq", None), P("dp", "seq"))
    return jax.shard_map(
        per_device, mesh=mesh, in_specs=in_specs, out_specs=out_specs, check_vma=False
    )
```

```python
import functools

import jax
import jax.numpy as jnp
from jax import lax
from jax.experimental import pallas as pl
from jax.experimental.pallas import tpu as pltpu
from jax.sharding import PartitionSpec as P

F32 = jnp.float32
BF16 = jnp.bfloat16
MESH = pl.DeviceIdType.MESH

H = 8
C = 128
S = 4
ROWS = S * C
D = 2048
MSG = C + 8
HALF = C // 2
ITERS = 4
FAR, SAME, NEAR = 3, 2, 5


def dot(a, b):
    return lax.dot_general(a, b, (((1,), (0,)), ((), ())), preferred_element_type=F32)


def dot_nt(a, b):
    return lax.dot_general(a, b, (((1,), (1,)), ((), ())), preferred_element_type=F32)


def dot_tn(a, b):
    return lax.dot_general(a, b, (((0,), (0,)), ((), ())), preferred_element_type=F32)


def kernel(
    tok_hbm, wq_hbm, k_hbm, v_hbm, ld_ref, reg_ref, g_hbm,
    mixed_hbm, qg_ref,
    tok, wq, kb, vb, gb, qb, mx,
    bs, el, wl, tl, ul, ll,
    loc, sib, tot, inbox, pre, pin, snd, st,
    gp, gin, zc, za, ya, fin,
    load_sem, out_sem,
    sib_send, sib_recv, fw_send, fw_recv, bk_send, bk_recv, st_send, st_recv,
    gs_send, gs_recv, zc_send, zc_recv, za_send, za_recv, fin_send, fin_recv,
):
    dp = lax.axis_index("dp")
    seq = lax.axis_index("seq")
    core = lax.rem(seq, 2)
    other = 1 - core
    chip = lax.div(seq, 2)
    zpos = lax.div(chip, 2)
    ylo = lax.rem(chip, 2)
    twin = (dp, chip * 2 + other)

    def at_chip(c):
        return (dp, c * 2 + core)

    def at_z(z):
        return (dp, (z * 2 + ylo) * 2 + core)

    z_up = lax.rem(zpos + 1, 4)
    z_down = lax.rem(zpos + 3, 4)
    z_far = lax.rem(zpos + 2, 4)

    def remote(src, dst, send, recv, device):
        return pltpu.make_async_remote_copy(
            src_ref=src, dst_ref=dst, send_sem=send, recv_sem=recv, device_id=device, device_id_type=MESH
        )

    loads = [
        pltpu.make_async_copy(src, dst, load_sem.at[n])
        for n, (src, dst) in enumerate(
            ((k_hbm, kb), (v_hbm, vb), (wq_hbm, wq), (tok_hbm, tok), (g_hbm, gb))
        )
    ]
    loads[0].start()
    loads[1].start()

    barrier = pltpu.get_barrier_semaphore()
    pl.semaphore_signal(barrier, inc=1, device_id=twin, device_id_type=MESH)
    for n in range(1, 8):
        pl.semaphore_signal(barrier, inc=1, device_id=at_chip(lax.rem(chip + n, 8)), device_id_type=MESH)
    near_same = (dp, (zpos * 2 + 1 - ylo) * 2 + core)
    near_other = (dp + 1 - 2 * lax.rem(dp, 2), (zpos * 2 + 1 - ylo) * 2 + core)

    def greet(device):
        pl.semaphore_signal(barrier, inc=1, device_id=device, device_id_type=MESH)

    @pl.when(core == 0)
    def _():
        for n in range(1, 8):
            for y in range(2):
                greet((lax.rem(dp + n, 8), (zpos * 2 + y) * 2))

    @pl.when(core == 1)
    def _():
        greet(near_other)
        for n in range(1, 4):
            for z in range(4):
                greet((lax.rem(dp + 2 * n, 8), (z * 2 + ylo) * 2 + 1))

    row_at = lax.broadcasted_iota(jnp.int32, (C, C), 0)
    col_at = lax.broadcasted_iota(jnp.int32, (C, C), 1)
    lower = row_at >= col_at
    eye = row_at == col_at

    xpos = lax.div(dp, 2)
    yhi = lax.rem(dp, 2)

    def head_at(n):
        return 2 * lax.rem(xpos + 1 + lax.div(n, 2), 4) + lax.rem(yhi + 1 + n, 2)

    def lanes(h):
        return pl.ds(pl.multiple_of(h * C, C), C)

    upper_ones = jnp.where(row_at <= col_at, 1.0, 0.0).astype(F32)
    for s in range(S):
        sums = lax.dot_general(
            ld_ref[:, s * C : (s + 1) * C], upper_ones, (((1,), (0,)), ((), ())),
            precision=lax.Precision.HIGHEST, preferred_element_type=F32,
        )
        for h in range(H):
            bs[h, s : s + 1, :] = sums[h : h + 1, :]

    loads[0].wait()
    loads[1].wait()
    for copy in (loads[4], loads[3], loads[2]):
        copy.start()

    def local_states(n, carry):
        h = head_at(n)
        m_sum = g_sum = None
        decay = None
        for s in range(S):
            rows = slice(s * C, (s + 1) * C)
            across = jnp.broadcast_to(bs[h, s : s + 1, :], (C, C))
            down = across.T
            e = jnp.exp(down)
            el[h, s] = e
            tail = jnp.exp(down[C - 1 : C, :] - down)
            k = kb[rows, lanes(h)]
            kt = (k.astype(F32) * tail).astype(BF16)
            vt = (vb[rows, lanes(h)].astype(F32) * tail).astype(BF16)
            m_new = dot_tn(vt, k)
            g_new = dot_tn(kt, k)
            ll[h, s, 0:C, :] = m_new
            ll[h, s, C : 2 * C, :] = g_new
            last = e[C - 1 : C, :]
            if s == 0:
                m_sum, g_sum, decay = m_new, g_new, last
            else:
                m_sum = last * m_sum + m_new
                g_sum = last * g_sum + g_new
                decay = decay * last
        tile = jnp.broadcast_to(decay, (8, C))
        loc[0, n, 0:C, :] = m_sum
        loc[0, n, C:MSG, :] = tile
        loc[1, n, 0:C, :] = g_sum
        loc[1, n, C:MSG, :] = tile
        return carry

    lax.fori_loop(0, 4, local_states, 0)

    pl.semaphore_wait(barrier, jnp.where(core == 0, 22, 21))

    def to_twin(r):
        four = pl.ds(4 * r, 4)
        return remote(loc.at[other, four], sib.at[four], sib_send.at[r], sib_recv.at[r], twin)

    to_twin(0).start()

    lax.fori_loop(4, H, local_states, 0)
    to_twin(1).start()

    loads[4].wait()

    def tables(h, carry):
        for s in range(S):
            rows = slice(s * C, (s + 1) * C)
            across = jnp.broadcast_to(bs[h, s : s + 1, :], (C, C))
            w = jnp.where(lower, jnp.exp(jnp.where(lower, across.T - across, 0.0)), 0.0)
            wl[h, s] = w
            k = kb[rows, lanes(h)]
            kf = k.astype(F32)
            square = jnp.broadcast_to(jnp.sum(kf * kf, axis=1, keepdims=True), (C, C))
            high = square.astype(BF16)
            low = (square - high.astype(F32)).astype(BF16)
            wb = w.astype(BF16)
            tl[h, s] = dot(jnp.concatenate([wb, wb], axis=1), jnp.concatenate([high, low], axis=0))
            ul[h, s] = (w * dot_nt(gb[rows, lanes(h)], vb[rows, lanes(h)])).astype(BF16)
        return carry

    def unit(r, u):
        return 4 * r + lax.div(u, 2), pl.ds(pl.multiple_of(lax.rem(u, 2) * HALF, HALF), HALF)

    def tiles(block):
        return block.reshape(HALF // 8, 8, C)

    def total(r, u):
        n, half = unit(r, u)
        mine_at = loc[core, n, C:MSG, :]
        sib_at = sib[n, C:MSG, :]
        first = core == 0
        by_mine = jnp.where(first, sib_at, 1.0)
        by_sib = jnp.where(first, 1.0, mine_at)
        tot[r, u, HALF : HALF + 8, :] = mine_at * sib_at
        mine, theirs = tiles(loc[core, n, half, :]), tiles(sib[n, half, :])
        tot[r, u, 0:HALF, :] = (by_mine[None] * mine + by_sib[None] * theirs).reshape(HALF, C)

    def forward(r, u):
        return remote(tot.at[r, u], inbox.at[r, chip], fw_send.at[r, u], fw_recv.at[r, chip], at_chip(u))

    def send_totals(r):
        def one(n, carry):
            u = lax.rem(chip + n, 8)
            total(r, u)
            forward(r, u).start()
            return carry

        lax.fori_loop(1, 8, one, 0)
        total(r, chip)
        inbox[r, chip] = tot[r, chip]

    def back(r, c):
        return remote(pre.at[r, c], pin.at[r, chip], bk_send.at[r, c], bk_recv.at[r, chip], at_chip(c))

    def prefix(r):
        state = jnp.zeros((HALF // 8, 8, C), F32)
        for c in range(8):
            pre[r, c] = state.reshape(HALF, C)

            @pl.when(c != chip)
            def _():
                back(r, c).start()
                remote(tot.at[r, c], inbox.at[r, c], fw_send.at[r, c], fw_recv.at[r, c], at_chip(c)).wait_recv()

            state = inbox[r, c, HALF : HALF + 8, :][None] * state + tiles(inbox[r, c, 0:HALF, :])
        pin[r, chip] = pre[r, chip]

    def hand_over(h):
        return remote(snd.at[h], st.at[core, h], st_send.at[h], st_recv.at[h], twin)

    def spread(r):
        def one(e, carry):
            n = 4 * r + e
            h = head_at(n)
            mine_at = loc[core, n, C:MSG, :]
            sib_at = sib[n, C:MSG, :]
            first = core == 0
            for part in range(2):
                u = 2 * e + part
                half = slice(part * HALF, (part + 1) * HALF)

                @pl.when(u != chip)
                def _():
                    remote(pre.at[r, u], pin.at[r, u], bk_send.at[r, u], bk_recv.at[r, u], at_chip(u)).wait_recv()

                base = tiles(pin[r, u])
                mine = mine_at[None] * base + tiles(loc[core, n, half, :])
                theirs = sib_at[None] * base + tiles(sib[n, half, :])
                snd[h, half, :] = jnp.where(first, mine, base).reshape(HALF, C)
                st[core, h, half, :] = jnp.where(first, base, theirs).reshape(HALF, C)
            hand_over(h).start()
            return carry

        lax.fori_loop(0, 4, one, 0)

    to_twin(0).wait_recv()
    send_totals(0)

    lax.fori_loop(0, H, tables, 0)

    prefix(0)

    loads[2].wait()
    loads[3].wait()
    for n in range(H // 2):
        if n == 2:
            to_twin(1).wait_recv()
            send_totals(1)
        block = dot(tok[...], wq[:, n * 2 * C : (n + 1) * 2 * C]).astype(BF16)
        qb[2 * n] = block[:, 0:C]
        qb[2 * n + 1] = block[:, C : 2 * C]

    spread(0)

    def apply(pq, pg, e, w, state, k):
        p = jnp.concatenate([pq, pg], axis=0).astype(BF16)
        scores = dot_nt(p, k)
        left = jnp.concatenate(
            [
                jnp.concatenate([e * pq, e * pg], axis=0).astype(BF16),
                jnp.concatenate([w * scores[0:C], w * scores[C : 2 * C]], axis=0).astype(BF16),
            ],
            axis=1,
        )
        y = dot(left, jnp.concatenate([state, k], axis=0))
        return y[0:C], y[C : 2 * C]

    def solve(n):
        h = head_at(n)
        ridge = reg_ref[h]
        remote(snd.at[h], st.at[other, h], st_send.at[h], st_recv.at[h], twin).wait_recv()
        m, g = st[0, h], st[1, h]
        trace = jnp.sum(jnp.sum(jnp.where(eye, g, 0.0), axis=0, keepdims=True), axis=1, keepdims=True)
        trace = jnp.broadcast_to(trace, (1, C))
        each = []
        for s in range(S):
            rows = slice(s * C, (s + 1) * C)
            e, w = el[h, s], wl[h, s]
            spans = e * trace + tl[h, s]
            trace = spans[C - 1 : C, :]
            half = 0.5 * spans
            center = ridge + half
            square = half * half
            alpha = 1.0 / center
            alphas, betas = [alpha], [None]
            for step in range(1, ITERS):
                factor = 0.5 if step == 1 else 0.25
                betas.append(factor * (half * alpha) * (half * alpha))
                alpha = 1.0 / (center - factor * square * alpha)
                alphas.append(alpha)
            each.append(dict(rows=rows, e=e, w=w, m=m.astype(BF16), g=g.astype(BF16), a=alphas, b=betas))
            if s + 1 < S:
                last = e[C - 1 : C, :]
                m = last * m + ll[h, s, 0:C, :]
                g = last * g + ll[h, s, C : 2 * C, :]
        for s, t in enumerate(each):
            k = kb[t["rows"], lanes(h)]
            grad = gb[t["rows"], lanes(h)].astype(F32)
            left = jnp.concatenate([(t["e"] * grad).astype(BF16), ul[h, s]], axis=1)
            rg = dot(left, jnp.concatenate([t["m"], k], axis=0))
            rq = qb[h, t["rows"], :].astype(F32)
            t.update(k=k, rq=rq, rg=rg, pq=rq, pg=rg, xq=t["a"][0] * rq, xg=t["a"][0] * rg)
        for step in range(1, ITERS):
            for t in each:
                yq, yg = apply(t["pq"], t["pg"], t["e"], t["w"], t["g"], t["k"])
                before, now, beta = t["a"][step - 1], t["a"][step], t["b"][step]
                for i, y in (("q", yq), ("g", yg)):
                    res = t["r" + i] - before * (ridge * t["p" + i] + y)
                    p = res + beta * t["p" + i]
                    t["r" + i], t["p" + i] = res, p
                    t["x" + i] = t["x" + i] + now * p
        solved = []
        for s, t in enumerate(each):
            scores = dot_nt(t["xq"].astype(BF16), t["k"])
            y = dot_nt((t["e"] * t["xq"]).astype(BF16), t["m"])
            y = y + dot((t["w"] * scores).astype(BF16), vb[t["rows"], lanes(h)])
            mx[t["rows"], lanes(h)] = y.astype(BF16)
            solved.append(t["xg"].T.astype(BF16))
        left = jnp.concatenate(solved, axis=1)
        for c in range(8):
            part = dot(left, tok[:, c * 2 * C : (c + 1) * 2 * C])
            gp[n, 0, c // 2, c % 2] = part[:, 0:C]
            gp[n, 1, c // 2, c % 2] = part[:, C : 2 * C]

    def out_copy(n):
        h = head_at(n)
        return pltpu.make_async_copy(mx.at[:, lanes(h)], mixed_hbm.at[:, lanes(h)], out_sem.at[n])

    def to_core(n):
        return remote(gp.at[n, other], gin.at[n], gs_send.at[n], gs_recv.at[n], twin)

    def far_up(n):
        return remote(gp.at[n, 0, z_far, 0], zc.at[n, 0], zc_send.at[n, 0], zc_recv.at[n, 0], at_z(z_up))

    def far_down(n):
        return remote(gp.at[n, 0, z_far, 1], zc.at[n, 1], zc_send.at[n, 1], zc_recv.at[n, 1], at_z(z_down))

    def near_up(n):
        return remote(gp.at[n, 0, z_up], za.at[n, 0], za_send.at[n, 0], za_recv.at[n, 0], at_z(z_up))

    def near_down(n):
        return remote(gp.at[n, 0, z_down], za.at[n, 1], za_send.at[n, 1], za_recv.at[n, 1], at_z(z_down))

    def finish_z(n, y):
        at = dp * 2 + ylo
        return remote(
            gp.at[n, 0, zpos, y], fin.at[at], fin_send.at[n, y], fin_recv.at[at], (head_at(n), (zpos * 2 + y) * 2)
        )

    def far_same(n):
        return remote(
            gp.at[n, 1, 0:2, ylo], zc.at[n], zc_send.at[n, 0], zc_recv.at[n, 0], near_same
        )

    def far_other(n):
        return remote(
            gp.at[n, 1, 2:4, ylo], zc.at[n + 1], zc_send.at[n, 1], zc_recv.at[n, 1], near_other
        )

    def send_other(n):
        return remote(gp.at[n, 1, :, 1 - ylo], ya.at[n], za_send.at[n, 0], za_recv.at[n, 0], near_other)

    def send_same(n):
        return remote(gp.at[n, 1, :, 1 - ylo], ya.at[n], za_send.at[n, 0], za_recv.at[n, 0], near_same)

    def finish_y(n, z):
        at = xpos * 4 + zpos
        return remote(
            gp.at[n, 1, z, ylo], fin.at[at], fin_send.at[n, z], fin_recv.at[at], (head_at(n), (z * 2 + ylo) * 2 + 1)
        )

    def odd(n):
        return lax.rem(n, 2) == 1

    def even(n):
        return lax.rem(n, 2) == 0

    def turn(i, carry):
        @pl.when(i == 1)
        def _():
            prefix(1)

        @pl.when(i == 3)
        def _():
            spread(1)

        @pl.when(i < H)
        def _():
            solve(i)
            to_core(i).start()
            out_copy(i).start()

        n1, n2, n3, n4 = i - 1, i - FAR, i - NEAR, i - SAME
        in1 = (i >= 1) & (i < H + 1)
        in2 = (i >= FAR) & (i < H + FAR)
        in3 = (i >= NEAR) & (i < H + NEAR)
        in4 = (i >= SAME) & (i < H + SAME)

        @pl.when(in1)
        def _():
            to_core(n1).wait_recv()
            gp[n1, core] = gp[n1, core] + gin[n1]

        @pl.when(in1 & (core == 0))
        def _():
            far_up(n1).start()
            far_down(n1).start()

        @pl.when(in2 & (core == 0))
        def _():
            far_up(n2).wait_recv()
            far_down(n2).wait_recv()
            gp[n2, 0, z_up, 0] = gp[n2, 0, z_up, 0] + zc[n2, 0]
            gp[n2, 0, z_down, 1] = gp[n2, 0, z_down, 1] + zc[n2, 1]
            near_up(n2).start()
            near_down(n2).start()

        @pl.when(in3 & (core == 0))
        def _():
            near_up(n3).wait_recv()
            near_down(n3).wait_recv()
            for y in range(2):
                gp[n3, 0, zpos, y] = gp[n3, 0, zpos, y] + za[n3, 0, y] + za[n3, 1, y]

                @pl.when((n3 < H - 1) | (ylo != y))
                def _():
                    finish_z(n3, y).start()

                @pl.when((n3 == H - 1) & (ylo == y))
                def _():
                    fin[dp * 2 + y] = gp[n3, 0, zpos, y]

        @pl.when(in1 & (core == 1) & even(n1))
        def _():
            far_same(n1).start()
            far_other(n1).start()

        @pl.when(in4 & (core == 1) & odd(n4))
        def _():
            far_other(n4 - 1).wait_recv()
            gp[n4, 1, 2:4, 1 - ylo] = gp[n4, 1, 2:4, 1 - ylo] + zc[n4]
            send_same(n4).start()

        @pl.when(in2 & (core == 1) & even(n2))
        def _():
            far_same(n2).wait_recv()
            gp[n2, 1, 0:2, 1 - ylo] = gp[n2, 1, 0:2, 1 - ylo] + zc[n2]
            send_other(n2).start()

        @pl.when(in3 & (core == 1) & odd(n3))
        def _():
            send_other(n3 - 1).wait_recv()
            send_same(n3).wait_recv()
            for z in range(4):
                gp[n3, 1, z, ylo] = gp[n3, 1, z, ylo] + ya[n3 - 1, z] + ya[n3, z]

                @pl.when((n3 < H - 1) | (zpos != z))
                def _():
                    finish_y(n3, z).start()

                @pl.when((n3 == H - 1) & (zpos == z))
                def _():
                    fin[xpos * 4 + z] = gp[n3, 1, z, ylo]

        return carry

    lax.fori_loop(0, H + NEAR, turn, 0)

    acc = None
    own = jnp.where(core == 0, dp * 2 + ylo, xpos * 4 + zpos)
    for source in range(16):

        @pl.when(own != source)
        def _():
            remote(gp.at[0, 0, 0, 0], fin.at[source], fin_send.at[0, 0], fin_recv.at[source], twin).wait_recv()

        acc = fin[source] if acc is None else acc + fin[source]
    qg_ref[...] = acc

    to_twin(0).wait_send()
    to_twin(1).wait_send()

    def drain(n, carry):
        @pl.when(n != chip)
        def _():
            for r in range(2):
                forward(r, n).wait_send()
                back(r, n).wait_send()

        hand_over(n).wait_send()
        out_copy(n).wait()
        to_core(n).wait_send()

        @pl.when(core == 0)
        def _():
            far_up(n).wait_send()
            far_down(n).wait_send()
            near_up(n).wait_send()
            near_down(n).wait_send()
            for y in range(2):

                @pl.when((n < H - 1) | (ylo != y))
                def _():
                    finish_z(n, y).wait_send()

        @pl.when((core == 1) & even(n))
        def _():
            far_same(n).wait_send()
            far_other(n).wait_send()
            send_other(n).wait_send()

        @pl.when((core == 1) & odd(n))
        def _():
            send_same(n).wait_send()
            for z in range(4):

                @pl.when((n < H - 1) | (zpos != z))
                def _():
                    finish_y(n, z).wait_send()

        return carry

    lax.fori_loop(0, H, drain, 0)


def per_device(tokens, w_query, keys, values, log_decay, regular, grad_out):
    dma = pltpu.SemaphoreType.DMA
    hbm = pl.BlockSpec(memory_space=pl.ANY)
    vmem = pl.BlockSpec(memory_space=pltpu.VMEM)
    smem = pl.BlockSpec(memory_space=pltpu.SMEM)
    mixed, query_grad = pl.pallas_call(
        kernel,
        out_shape=(
            jax.ShapeDtypeStruct((ROWS, H * C), BF16),
            jax.ShapeDtypeStruct((C, C), F32),
        ),
        in_specs=[hbm, hbm, hbm, hbm, vmem, smem, hbm],
        out_specs=(hbm, vmem),
        scratch_shapes=[
            pltpu.VMEM((ROWS, D), BF16),
            pltpu.VMEM((D, H * C), BF16),
            pltpu.VMEM((ROWS, H * C), BF16),
            pltpu.VMEM((ROWS, H * C), BF16),
            pltpu.VMEM((ROWS, H * C), BF16),
            pltpu.VMEM((H, ROWS, C), BF16),
            pltpu.VMEM((ROWS, H * C), BF16),
            pltpu.VMEM((H, S, C), F32),
            pltpu.VMEM((H, S, C, C), F32),
            pltpu.VMEM((H, S, C, C), F32),
            pltpu.VMEM((H, S, C, C), F32),
            pltpu.VMEM((H, S, C, C), BF16),
            pltpu.VMEM((H, S, 2 * C, C), F32),
            pltpu.VMEM((2, H, MSG, C), F32),
            pltpu.VMEM((H, MSG, C), F32),
            pltpu.VMEM((2, 8, HALF + 8, C), F32),
            pltpu.VMEM((2, 8, HALF + 8, C), F32),
            pltpu.VMEM((2, 8, HALF, C), F32),
            pltpu.VMEM((2, 8, HALF, C), F32),
            pltpu.VMEM((H, C, C), F32),
            pltpu.VMEM((2, H, C, C), F32),
            pltpu.VMEM((H, 2, 4, 2, C, C), F32),
            pltpu.VMEM((H, 4, 2, C, C), F32),
            pltpu.VMEM((H, 2, C, C), F32),
            pltpu.VMEM((H, 2, 2, C, C), F32),
            pltpu.VMEM((H, 4, C, C), F32),
            pltpu.VMEM((16, C, C), F32),
            dma((5,)),
            dma((H,)),
            dma((2,)),
            dma((2,)),
            dma((2, 8)),
            dma((2, 8)),
            dma((2, 8)),
            dma((2, 8)),
            dma((H,)),
            dma((H,)),
            dma((H,)),
            dma((H,)),
            dma((H, 2)),
            dma((H, 2)),
            dma((H, 2)),
            dma((H, 2)),
            dma((H, 4)),
            dma((16,)),
        ],
        compiler_params=pltpu.CompilerParams(
            collective_id=0, has_side_effects=True, vmem_limit_bytes=60 * 2**20
        ),
    )(
        tokens.reshape(ROWS, D),
        w_query,
        keys.reshape(ROWS, H * C),
        values.reshape(ROWS, H * C),
        log_decay.reshape(H, ROWS),
        regular,
        grad_out.reshape(ROWS, H * C),
    )
    parts = 4
    step = ROWS // parts

    def move(a_ref, b_ref, c_ref, d_ref, held, sums, sem_in, sem_out):
        def a_copy(n):
            rows = pl.ds(n * step, step)
            return (
                pltpu.make_async_copy(a_ref.at[rows], held.at[rows], sem_in.at[n]),
                pltpu.make_async_copy(held.at[rows], c_ref.at[rows], sem_out.at[n]),
            )

        pairs = [a_copy(n) for n in range(parts)]
        pairs.append(
            (
                pltpu.make_async_copy(b_ref, sums, sem_in.at[parts]),
                pltpu.make_async_copy(sums, d_ref, sem_out.at[parts]),
            )
        )
        for come, _ in pairs:
            come.start()
        for come, go in pairs:
            come.wait()
            go.start()
        for _, go in pairs:
            go.wait()

    mixed, query_grad = pl.pallas_call(
        move,
        out_shape=(jax.ShapeDtypeStruct(mixed.shape, BF16), jax.ShapeDtypeStruct(query_grad.shape, F32)),
        in_specs=[hbm, hbm],
        out_specs=(hbm, hbm),
        scratch_shapes=[
            pltpu.VMEM((ROWS, H * C), BF16),
            pltpu.VMEM((C, C), F32),
            dma((parts + 1,)),
            dma((parts + 1,)),
        ],
    )(mixed, query_grad)
    return mixed.reshape(1, ROWS, H * C), query_grad


def solution(mesh):
    in_specs = (
        P("dp", "seq", None),
        P(),
        P("dp", "seq", None),
        P("dp", "seq", None),
        P("dp", None, "seq"),
        P(),
        P("dp", "seq", None),
    )
    out_specs = (P("dp", "seq", None), P("dp", "seq"))
    return jax.shard_map(
        per_device, mesh=mesh, in_specs=in_specs, out_specs=out_specs, check_vma=False
    )
```

```python
import functools

import jax
import jax.numpy as jnp
from jax import lax
from jax.experimental import pallas as pl
from jax.experimental.pallas import tpu as pltpu
from jax.sharding import PartitionSpec as P

F32 = jnp.float32
BF16 = jnp.bfloat16
MESH = pl.DeviceIdType.MESH

H = 8
C = 128
S = 4
ROWS = S * C
D = 2048
MSG = C + 8
HALF = C // 2
ITERS = 4
FAR, SAME, NEAR = 3, 2, 5


def dot(a, b):
    return lax.dot_general(a, b, (((1,), (0,)), ((), ())), preferred_element_type=F32)


def dot_nt(a, b):
    return lax.dot_general(a, b, (((1,), (1,)), ((), ())), preferred_element_type=F32)


def dot_tn(a, b):
    return lax.dot_general(a, b, (((0,), (0,)), ((), ())), preferred_element_type=F32)


def kernel(
    tok_hbm, wq_hbm, k_hbm, v_hbm, ld_ref, reg_ref, g_hbm,
    mixed_hbm, qg_ref,
    tok, wq, kb, vb, gb, qb, mx,
    bs, el, wl, tl, ul, ll,
    loc, sib, tot, inbox, pre, pin, snd, st,
    gp, gin, zc, za, ya, fin,
    load_sem, out_sem,
    sib_send, sib_recv, fw_send, fw_recv, bk_send, bk_recv, st_send, st_recv,
    gs_send, gs_recv, zc_send, zc_recv, za_send, za_recv, fin_send, fin_recv,
):
    dp = lax.axis_index("dp")
    seq = lax.axis_index("seq")
    core = lax.rem(seq, 2)
    other = 1 - core
    chip = lax.div(seq, 2)
    zpos = lax.div(chip, 2)
    ylo = lax.rem(chip, 2)
    twin = (dp, chip * 2 + other)

    def at_chip(c):
        return (dp, c * 2 + core)

    def at_z(z):
        return (dp, (z * 2 + ylo) * 2 + core)

    z_up = lax.rem(zpos + 1, 4)
    z_down = lax.rem(zpos + 3, 4)
    z_far = lax.rem(zpos + 2, 4)

    def remote(src, dst, send, recv, device):
        return pltpu.make_async_remote_copy(
            src_ref=src, dst_ref=dst, send_sem=send, recv_sem=recv, device_id=device, device_id_type=MESH
        )

    loads = [
        pltpu.make_async_copy(src, dst, load_sem.at[n])
        for n, (src, dst) in enumerate(
            ((k_hbm, kb), (v_hbm, vb), (wq_hbm, wq), (tok_hbm, tok), (g_hbm, gb))
        )
    ]
    loads[0].start()
    loads[1].start()

    barrier = pltpu.get_barrier_semaphore()
    pl.semaphore_signal(barrier, inc=1, device_id=twin, device_id_type=MESH)
    for n in range(1, 8):
        pl.semaphore_signal(barrier, inc=1, device_id=at_chip(lax.rem(chip + n, 8)), device_id_type=MESH)
    near_same = (dp, (zpos * 2 + 1 - ylo) * 2 + core)
    near_other = (dp + 1 - 2 * lax.rem(dp, 2), (zpos * 2 + 1 - ylo) * 2 + core)

    def greet(device):
        pl.semaphore_signal(barrier, inc=1, device_id=device, device_id_type=MESH)

    @pl.when(core == 0)
    def _():
        for n in range(1, 8):
            for y in range(2):
                greet((lax.rem(dp + n, 8), (zpos * 2 + y) * 2))

    @pl.when(core == 1)
    def _():
        greet(near_other)
        for n in range(1, 4):
            for z in range(4):
                greet((lax.rem(dp + 2 * n, 8), (z * 2 + ylo) * 2 + 1))

    row_at = lax.broadcasted_iota(jnp.int32, (C, C), 0)
    col_at = lax.broadcasted_iota(jnp.int32, (C, C), 1)
    lower = row_at >= col_at
    eye = row_at == col_at

    xpos = lax.div(dp, 2)
    yhi = lax.rem(dp, 2)

    def head_at(n):
        return 2 * lax.rem(xpos + 1 + lax.div(n, 2), 4) + lax.rem(yhi + 1 + n, 2)

    def lanes(h):
        return pl.ds(pl.multiple_of(h * C, C), C)

    upper_ones = jnp.where(row_at <= col_at, 1.0, 0.0).astype(F32)
    for s in range(S):
        sums = lax.dot_general(
            ld_ref[:, s * C : (s + 1) * C], upper_ones, (((1,), (0,)), ((), ())),
            precision=lax.Precision.HIGHEST, preferred_element_type=F32,
        )
        for h in range(H):
            bs[h, s : s + 1, :] = sums[h : h + 1, :]

    loads[0].wait()
    loads[1].wait()
    for copy in (loads[4], loads[3], loads[2]):
        copy.start()

    def local_states(n, carry):
        h = head_at(n)
        m_sum = g_sum = None
        decay = None
        for s in range(S):
            rows = slice(s * C, (s + 1) * C)
            across = jnp.broadcast_to(bs[h, s : s + 1, :], (C, C))
            down = across.T
            e = jnp.exp(down)
            el[h, s] = e
            tail = jnp.exp(down[C - 1 : C, :] - down)
            k = kb[rows, lanes(h)]
            kt = (k.astype(F32) * tail).astype(BF16)
            vt = (vb[rows, lanes(h)].astype(F32) * tail).astype(BF16)
            m_new = dot_tn(vt, k)
            g_new = dot_tn(kt, k)
            ll[h, s, 0:C, :] = m_new
            ll[h, s, C : 2 * C, :] = g_new
            last = e[C - 1 : C, :]
            if s == 0:
                m_sum, g_sum, decay = m_new, g_new, last
            else:
                m_sum = last * m_sum + m_new
                g_sum = last * g_sum + g_new
                decay = decay * last
        tile = jnp.broadcast_to(decay, (8, C))
        loc[0, n, 0:C, :] = m_sum
        loc[0, n, C:MSG, :] = tile
        loc[1, n, 0:C, :] = g_sum
        loc[1, n, C:MSG, :] = tile
        return carry

    lax.fori_loop(0, 4, local_states, 0)

    pl.semaphore_wait(barrier, jnp.where(core == 0, 22, 21))

    def to_twin(r):
        four = pl.ds(4 * r, 4)
        return remote(loc.at[other, four], sib.at[four], sib_send.at[r], sib_recv.at[r], twin)

    to_twin(0).start()

    lax.fori_loop(4, H, local_states, 0)
    to_twin(1).start()

    loads[4].wait()

    def tables(h, carry):
        for s in range(S):
            rows = slice(s * C, (s + 1) * C)
            across = jnp.broadcast_to(bs[h, s : s + 1, :], (C, C))
            w = jnp.where(lower, jnp.exp(jnp.where(lower, across.T - across, 0.0)), 0.0)
            wl[h, s] = w
            k = kb[rows, lanes(h)]
            kf = k.astype(F32)
            square = jnp.broadcast_to(jnp.sum(kf * kf, axis=1, keepdims=True), (C, C))
            high = square.astype(BF16)
            low = (square - high.astype(F32)).astype(BF16)
            wb = w.astype(BF16)
            tl[h, s] = dot(jnp.concatenate([wb, wb], axis=1), jnp.concatenate([high, low], axis=0))
            ul[h, s] = (w * dot_nt(gb[rows, lanes(h)], vb[rows, lanes(h)])).astype(BF16)
        return carry

    def unit(r, u):
        return 4 * r + lax.div(u, 2), pl.ds(pl.multiple_of(lax.rem(u, 2) * HALF, HALF), HALF)

    def tiles(block):
        return block.reshape(HALF // 8, 8, C)

    def total(r, u):
        n, half = unit(r, u)
        mine_at = loc[core, n, C:MSG, :]
        sib_at = sib[n, C:MSG, :]
        first = core == 0
        by_mine = jnp.where(first, sib_at, 1.0)
        by_sib = jnp.where(first, 1.0, mine_at)
        tot[r, u, HALF : HALF + 8, :] = mine_at * sib_at
        mine, theirs = tiles(loc[core, n, half, :]), tiles(sib[n, half, :])
        tot[r, u, 0:HALF, :] = (by_mine[None] * mine + by_sib[None] * theirs).reshape(HALF, C)

    def forward(r, u):
        return remote(tot.at[r, u], inbox.at[r, chip], fw_send.at[r, u], fw_recv.at[r, chip], at_chip(u))

    def send_totals(r):
        def one(n, carry):
            u = lax.rem(chip + n, 8)
            total(r, u)
            forward(r, u).start()
            return carry

        lax.fori_loop(1, 8, one, 0)
        total(r, chip)
        inbox[r, chip] = tot[r, chip]

    def back(r, c):
        return remote(pre.at[r, c], pin.at[r, chip], bk_send.at[r, c], bk_recv.at[r, chip], at_chip(c))

    def prefix(r):
        state = jnp.zeros((HALF // 8, 8, C), F32)
        for c in range(8):
            pre[r, c] = state.reshape(HALF, C)

            @pl.when(c != chip)
            def _():
                back(r, c).start()
                remote(tot.at[r, c], inbox.at[r, c], fw_send.at[r, c], fw_recv.at[r, c], at_chip(c)).wait_recv()

            state = inbox[r, c, HALF : HALF + 8, :][None] * state + tiles(inbox[r, c, 0:HALF, :])
        pin[r, chip] = pre[r, chip]

    def hand_over(h):
        return remote(snd.at[h], st.at[core, h], st_send.at[h], st_recv.at[h], twin)

    def spread(r):
        def one(e, carry):
            n = 4 * r + e
            h = head_at(n)
            mine_at = loc[core, n, C:MSG, :]
            sib_at = sib[n, C:MSG, :]
            first = core == 0
            for part in range(2):
                u = 2 * e + part
                half = slice(part * HALF, (part + 1) * HALF)

                @pl.when(u != chip)
                def _():
                    remote(pre.at[r, u], pin.at[r, u], bk_send.at[r, u], bk_recv.at[r, u], at_chip(u)).wait_recv()

                base = tiles(pin[r, u])
                mine = mine_at[None] * base + tiles(loc[core, n, half, :])
                theirs = sib_at[None] * base + tiles(sib[n, half, :])
                snd[h, half, :] = jnp.where(first, mine, base).reshape(HALF, C)
                st[core, h, half, :] = jnp.where(first, base, theirs).reshape(HALF, C)
            hand_over(h).start()
            return carry

        lax.fori_loop(0, 4, one, 0)

    to_twin(0).wait_recv()
    send_totals(0)

    lax.fori_loop(0, H, tables, 0)

    prefix(0)

    loads[2].wait()
    loads[3].wait()
    for n in range(H // 2):
        if n == 1:
            to_twin(1).wait_recv()
            send_totals(1)
        block = dot(tok[...], wq[:, n * 2 * C : (n + 1) * 2 * C]).astype(BF16)
        qb[2 * n] = block[:, 0:C]
        qb[2 * n + 1] = block[:, C : 2 * C]

    spread(0)

    def apply(pq, pg, e, w, state, k):
        p = jnp.concatenate([pq, pg], axis=0).astype(BF16)
        scores = dot_nt(p, k)
        left = jnp.concatenate(
            [
                jnp.concatenate([e * pq, e * pg], axis=0).astype(BF16),
                jnp.concatenate([w * scores[0:C], w * scores[C : 2 * C]], axis=0).astype(BF16),
            ],
            axis=1,
        )
        y = dot(left, jnp.concatenate([state, k], axis=0))
        return y[0:C], y[C : 2 * C]

    def solve(n):
        h = head_at(n)
        ridge = reg_ref[h]
        remote(snd.at[h], st.at[other, h], st_send.at[h], st_recv.at[h], twin).wait_recv()
        m, g = st[0, h], st[1, h]
        trace = jnp.sum(jnp.sum(jnp.where(eye, g, 0.0), axis=0, keepdims=True), axis=1, keepdims=True)
        trace = jnp.broadcast_to(trace, (1, C))
        each = []
        for s in range(S):
            rows = slice(s * C, (s + 1) * C)
            e, w = el[h, s], wl[h, s]
            spans = e * trace + tl[h, s]
            trace = spans[C - 1 : C, :]
            half = 0.5 * spans
            center = ridge + half
            square = half * half
            alpha = 1.0 / center
            alphas, betas = [alpha], [None]
            for step in range(1, ITERS):
                factor = 0.5 if step == 1 else 0.25
                betas.append(factor * (half * alpha) * (half * alpha))
                alpha = 1.0 / (center - factor * square * alpha)
                alphas.append(alpha)
            each.append(dict(rows=rows, e=e, w=w, m=m.astype(BF16), g=g.astype(BF16), a=alphas, b=betas))
            if s + 1 < S:
                last = e[C - 1 : C, :]
                m = last * m + ll[h, s, 0:C, :]
                g = last * g + ll[h, s, C : 2 * C, :]
        for s, t in enumerate(each):
            k = kb[t["rows"], lanes(h)]
            grad = gb[t["rows"], lanes(h)].astype(F32)
            left = jnp.concatenate([(t["e"] * grad).astype(BF16), ul[h, s]], axis=1)
            rg = dot(left, jnp.concatenate([t["m"], k], axis=0))
            rq = qb[h, t["rows"], :].astype(F32)
            t.update(k=k, rq=rq, rg=rg, pq=rq, pg=rg, xq=t["a"][0] * rq, xg=t["a"][0] * rg)
        for step in range(1, ITERS):
            for t in each:
                yq, yg = apply(t["pq"], t["pg"], t["e"], t["w"], t["g"], t["k"])
                before, now, beta = t["a"][step - 1], t["a"][step], t["b"][step]
                for i, y in (("q", yq), ("g", yg)):
                    res = t["r" + i] - before * (ridge * t["p" + i] + y)
                    p = res + beta * t["p" + i]
                    t["r" + i], t["p" + i] = res, p
                    t["x" + i] = t["x" + i] + now * p
        solved = []
        for s, t in enumerate(each):
            scores = dot_nt(t["xq"].astype(BF16), t["k"])
            y = dot_nt((t["e"] * t["xq"]).astype(BF16), t["m"])
            y = y + dot((t["w"] * scores).astype(BF16), vb[t["rows"], lanes(h)])
            mx[t["rows"], lanes(h)] = y.astype(BF16)
            solved.append(t["xg"].T.astype(BF16))
        left = jnp.concatenate(solved, axis=1)
        for c in range(8):
            part = dot(left, tok[:, c * 2 * C : (c + 1) * 2 * C])
            gp[n, 0, c // 2, c % 2] = part[:, 0:C]
            gp[n, 1, c // 2, c % 2] = part[:, C : 2 * C]

    def out_copy(n):
        h = head_at(n)
        return pltpu.make_async_copy(mx.at[:, lanes(h)], mixed_hbm.at[:, lanes(h)], out_sem.at[n])

    def to_core(n):
        return remote(gp.at[n, other], gin.at[n], gs_send.at[n], gs_recv.at[n], twin)

    def far_up(n):
        return remote(gp.at[n, 0, z_far, 0], zc.at[n, 0], zc_send.at[n, 0], zc_recv.at[n, 0], at_z(z_up))

    def far_down(n):
        return remote(gp.at[n, 0, z_far, 1], zc.at[n, 1], zc_send.at[n, 1], zc_recv.at[n, 1], at_z(z_down))

    def near_up(n):
        return remote(gp.at[n, 0, z_up], za.at[n, 0], za_send.at[n, 0], za_recv.at[n, 0], at_z(z_up))

    def near_down(n):
        return remote(gp.at[n, 0, z_down], za.at[n, 1], za_send.at[n, 1], za_recv.at[n, 1], at_z(z_down))

    def finish_z(n, y):
        at = dp * 2 + ylo
        return remote(
            gp.at[n, 0, zpos, y], fin.at[at], fin_send.at[n, y], fin_recv.at[at], (head_at(n), (zpos * 2 + y) * 2)
        )

    def far_same(n):
        return remote(
            gp.at[n, 1, 0:2, ylo], zc.at[n], zc_send.at[n, 0], zc_recv.at[n, 0], near_same
        )

    def far_other(n):
        return remote(
            gp.at[n, 1, 2:4, ylo], zc.at[n + 1], zc_send.at[n, 1], zc_recv.at[n, 1], near_other
        )

    def send_other(n):
        return remote(gp.at[n, 1, :, 1 - ylo], ya.at[n], za_send.at[n, 0], za_recv.at[n, 0], near_other)

    def send_same(n):
        return remote(gp.at[n, 1, :, 1 - ylo], ya.at[n], za_send.at[n, 0], za_recv.at[n, 0], near_same)

    def finish_y(n, z):
        at = xpos * 4 + zpos
        return remote(
            gp.at[n, 1, z, ylo], fin.at[at], fin_send.at[n, z], fin_recv.at[at], (head_at(n), (z * 2 + ylo) * 2 + 1)
        )

    def odd(n):
        return lax.rem(n, 2) == 1

    def even(n):
        return lax.rem(n, 2) == 0

    def turn(i, carry):
        @pl.when(i == 1)
        def _():
            prefix(1)

        @pl.when(i == 3)
        def _():
            spread(1)

        @pl.when(i < H)
        def _():
            solve(i)
            to_core(i).start()
            out_copy(i).start()

        n1, n2, n3, n4 = i - 1, i - FAR, i - NEAR, i - SAME
        in1 = (i >= 1) & (i < H + 1)
        in2 = (i >= FAR) & (i < H + FAR)
        in3 = (i >= NEAR) & (i < H + NEAR)
        in4 = (i >= SAME) & (i < H + SAME)

        @pl.when(in1)
        def _():
            to_core(n1).wait_recv()
            gp[n1, core] = gp[n1, core] + gin[n1]

        @pl.when(in1 & (core == 0))
        def _():
            far_up(n1).start()
            far_down(n1).start()

        @pl.when(in2 & (core == 0))
        def _():
            far_up(n2).wait_recv()
            far_down(n2).wait_recv()
            gp[n2, 0, z_up, 0] = gp[n2, 0, z_up, 0] + zc[n2, 0]
            gp[n2, 0, z_down, 1] = gp[n2, 0, z_down, 1] + zc[n2, 1]
            near_up(n2).start()
            near_down(n2).start()

        @pl.when(in3 & (core == 0))
        def _():
            near_up(n3).wait_recv()
            near_down(n3).wait_recv()
            for y in range(2):
                gp[n3, 0, zpos, y] = gp[n3, 0, zpos, y] + za[n3, 0, y] + za[n3, 1, y]

                @pl.when((n3 < H - 1) | (ylo != y))
                def _():
                    finish_z(n3, y).start()

                @pl.when((n3 == H - 1) & (ylo == y))
                def _():
                    fin[dp * 2 + y] = gp[n3, 0, zpos, y]

        @pl.when(in1 & (core == 1) & even(n1))
        def _():
            far_same(n1).start()
            far_other(n1).start()

        @pl.when(in4 & (core == 1) & odd(n4))
        def _():
            far_other(n4 - 1).wait_recv()
            gp[n4, 1, 2:4, 1 - ylo] = gp[n4, 1, 2:4, 1 - ylo] + zc[n4]
            send_same(n4).start()

        @pl.when(in2 & (core == 1) & even(n2))
        def _():
            far_same(n2).wait_recv()
            gp[n2, 1, 0:2, 1 - ylo] = gp[n2, 1, 0:2, 1 - ylo] + zc[n2]
            send_other(n2).start()

        @pl.when(in3 & (core == 1) & odd(n3))
        def _():
            send_other(n3 - 1).wait_recv()
            send_same(n3).wait_recv()
            for z in range(4):
                gp[n3, 1, z, ylo] = gp[n3, 1, z, ylo] + ya[n3 - 1, z] + ya[n3, z]

                @pl.when((n3 < H - 1) | (zpos != z))
                def _():
                    finish_y(n3, z).start()

                @pl.when((n3 == H - 1) & (zpos == z))
                def _():
                    fin[xpos * 4 + z] = gp[n3, 1, z, ylo]

        return carry

    lax.fori_loop(0, H + NEAR, turn, 0)

    acc = None
    own = jnp.where(core == 0, dp * 2 + ylo, xpos * 4 + zpos)
    for source in range(16):

        @pl.when(own != source)
        def _():
            remote(gp.at[0, 0, 0, 0], fin.at[source], fin_send.at[0, 0], fin_recv.at[source], twin).wait_recv()

        acc = fin[source] if acc is None else acc + fin[source]
    qg_ref[...] = acc

    to_twin(0).wait_send()
    to_twin(1).wait_send()

    def drain(n, carry):
        @pl.when(n != chip)
        def _():
            for r in range(2):
                forward(r, n).wait_send()
                back(r, n).wait_send()

        hand_over(n).wait_send()
        out_copy(n).wait()
        to_core(n).wait_send()

        @pl.when(core == 0)
        def _():
            far_up(n).wait_send()
            far_down(n).wait_send()
            near_up(n).wait_send()
            near_down(n).wait_send()
            for y in range(2):

                @pl.when((n < H - 1) | (ylo != y))
                def _():
                    finish_z(n, y).wait_send()

        @pl.when((core == 1) & even(n))
        def _():
            far_same(n).wait_send()
            far_other(n).wait_send()
            send_other(n).wait_send()

        @pl.when((core == 1) & odd(n))
        def _():
            send_same(n).wait_send()
            for z in range(4):

                @pl.when((n < H - 1) | (zpos != z))
                def _():
                    finish_y(n, z).wait_send()

        return carry

    lax.fori_loop(0, H, drain, 0)


def per_device(tokens, w_query, keys, values, log_decay, regular, grad_out):
    dma = pltpu.SemaphoreType.DMA
    hbm = pl.BlockSpec(memory_space=pl.ANY)
    vmem = pl.BlockSpec(memory_space=pltpu.VMEM)
    smem = pl.BlockSpec(memory_space=pltpu.SMEM)
    mixed, query_grad = pl.pallas_call(
        kernel,
        out_shape=(
            jax.ShapeDtypeStruct((ROWS, H * C), BF16),
            jax.ShapeDtypeStruct((C, C), F32),
        ),
        in_specs=[hbm, hbm, hbm, hbm, vmem, smem, hbm],
        out_specs=(hbm, vmem),
        scratch_shapes=[
            pltpu.VMEM((ROWS, D), BF16),
            pltpu.VMEM((D, H * C), BF16),
            pltpu.VMEM((ROWS, H * C), BF16),
            pltpu.VMEM((ROWS, H * C), BF16),
            pltpu.VMEM((ROWS, H * C), BF16),
            pltpu.VMEM((H, ROWS, C), BF16),
            pltpu.VMEM((ROWS, H * C), BF16),
            pltpu.VMEM((H, S, C), F32),
            pltpu.VMEM((H, S, C, C), F32),
            pltpu.VMEM((H, S, C, C), F32),
            pltpu.VMEM((H, S, C, C), F32),
            pltpu.VMEM((H, S, C, C), BF16),
            pltpu.VMEM((H, S, 2 * C, C), F32),
            pltpu.VMEM((2, H, MSG, C), F32),
            pltpu.VMEM((H, MSG, C), F32),
            pltpu.VMEM((2, 8, HALF + 8, C), F32),
            pltpu.VMEM((2, 8, HALF + 8, C), F32),
            pltpu.VMEM((2, 8, HALF, C), F32),
            pltpu.VMEM((2, 8, HALF, C), F32),
            pltpu.VMEM((H, C, C), F32),
            pltpu.VMEM((2, H, C, C), F32),
            pltpu.VMEM((H, 2, 4, 2, C, C), F32),
            pltpu.VMEM((H, 4, 2, C, C), F32),
            pltpu.VMEM((H, 2, C, C), F32),
            pltpu.VMEM((H, 2, 2, C, C), F32),
            pltpu.VMEM((H, 4, C, C), F32),
            pltpu.VMEM((16, C, C), F32),
            dma((5,)),
            dma((H,)),
            dma((2,)),
            dma((2,)),
            dma((2, 8)),
            dma((2, 8)),
            dma((2, 8)),
            dma((2, 8)),
            dma((H,)),
            dma((H,)),
            dma((H,)),
            dma((H,)),
            dma((H, 2)),
            dma((H, 2)),
            dma((H, 2)),
            dma((H, 2)),
            dma((H, 4)),
            dma((16,)),
        ],
        compiler_params=pltpu.CompilerParams(
            collective_id=0, has_side_effects=True, vmem_limit_bytes=60 * 2**20
        ),
    )(
        tokens.reshape(ROWS, D),
        w_query,
        keys.reshape(ROWS, H * C),
        values.reshape(ROWS, H * C),
        log_decay.reshape(H, ROWS),
        regular,
        grad_out.reshape(ROWS, H * C),
    )
    parts = 4
    step = ROWS // parts

    def move(a_ref, b_ref, c_ref, d_ref, held, sums, sem_in, sem_out):
        def a_copy(n):
            rows = pl.ds(n * step, step)
            return (
                pltpu.make_async_copy(a_ref.at[rows], held.at[rows], sem_in.at[n]),
                pltpu.make_async_copy(held.at[rows], c_ref.at[rows], sem_out.at[n]),
            )

        pairs = [a_copy(n) for n in range(parts)]
        pairs.append(
            (
                pltpu.make_async_copy(b_ref, sums, sem_in.at[parts]),
                pltpu.make_async_copy(sums, d_ref, sem_out.at[parts]),
            )
        )
        for come, _ in pairs:
            come.start()
        for come, go in pairs:
            come.wait()
            go.start()
        for _, go in pairs:
            go.wait()

    mixed, query_grad = pl.pallas_call(
        move,
        out_shape=(jax.ShapeDtypeStruct(mixed.shape, BF16), jax.ShapeDtypeStruct(query_grad.shape, F32)),
        in_specs=[hbm, hbm],
        out_specs=(hbm, hbm),
        scratch_shapes=[
            pltpu.VMEM((ROWS, H * C), BF16),
            pltpu.VMEM((C, C), F32),
            dma((parts + 1,)),
            dma((parts + 1,)),
        ],
    )(mixed, query_grad)
    return mixed.reshape(1, ROWS, H * C), query_grad


def solution(mesh):
    in_specs = (
        P("dp", "seq", None),
        P(),
        P("dp", "seq", None),
        P("dp", "seq", None),
        P("dp", None, "seq"),
        P(),
        P("dp", "seq", None),
    )
    out_specs = (P("dp", "seq", None), P("dp", "seq"))
    return jax.shard_map(
        per_device, mesh=mesh, in_specs=in_specs, out_specs=out_specs, check_vma=False
    )
```
